128 devices in a mesh: prompt: 8 (over z_lo, x), resp: 16 (over z_hi, y, core).
Axes of the slice: x: 4, y: 4, z: 4 (z_hi: 2, z_lo: 2; z = z_hi * 2 + z_lo), core: 2. Of those that a mesh axis runs over, the one named last changes fastest.
Arguments:
- queries: bfloat16 [8, 2048, 8192], P('prompt', 'resp')
- keys: bfloat16 [8, 2048, 1024], P('prompt', 'resp')
- values: bfloat16 [8, 2048, 1024], P('prompt', 'resp'), may hold values from -6 to 6
- prefix_keys: bfloat16 [8, 512, 1024], P('prompt', 'resp')
- prefix_values: bfloat16 [8, 512, 1024], P('prompt', 'resp'), may hold values from -6 to 6
- out_grad: bfloat16 [8, 2048, 8192], P('prompt', 'resp'), may hold values from -6 to 6
- q_gain: float32 [128], replicated, may hold values from 0.25 to 1.75
- k_gain: float32 [128], replicated, may hold values from 0.25 to 1.75
- lengths: int32 [8, 16], P('prompt'), may hold values from 1 to 128, as said below
- assign: int32 [8, 16], P('prompt'), may hold values from 0 to 15, as said below
Outputs:
- attention: bfloat16 [8, 2048, 8192], P('prompt', 'resp')
- grad_queries: bfloat16 [8, 2048, 8192], P('prompt', 'resp')
- grad_keys: bfloat16 [8, 2048, 1024], P('prompt', 'resp')
- grad_values: bfloat16 [8, 2048, 1024], P('prompt', 'resp')
- prefix_grad_keys: bfloat16 [8, 512, 1024], P('prompt', 'resp')
- prefix_grad_values: bfloat16 [8, 512, 1024], P('prompt', 'resp')
- q_gain_grad: float32 [128], replicated
- k_gain_grad: float32 [128], replicated
The draws below stay inside these ranges and needn't reach their ends.
Inputs may be any that keep to these rules, and one draw needn't show every extreme that they name: `assign`: each device of a group holds exactly 1 responses. `lengths`: the responses of one device fill at most its 128 slots; in each group one device's slots are all used.
All inputs are finite; a program needn't handle non-finite values.
Results may differ from the reference program's by a relative error of at most 0.035.
The reference program's roundings to bfloat16 on the way count: a program that leaves them out, or rounds other values in their place, can miss the bound.
Values may be sent and summed in bfloat16 or wider, within the bound.
No kernel may reach another device: no remote copies, remote signals or barrier semaphores. Data moves between devices by JAX's collectives and lax.ppermute only.
A program may use at most 128 MiB of HBM per device.

```python
import math
import jax
import jax.numpy as jnp
from jax import lax

HEAD_DIM = 128
RESPONSES = 16
GROUPS = 8
PREFIX = 512
SLOTS = 2048
PER_DEV = 1
MOST = 128
QW = 8192
KVW = 1024
N_RESP = 16


def scaled_rows(rng_key, rows, width, head_dim, spread):
    first, second, third = jax.random.split(rng_key, 3)
    row_scale = jnp.exp(jax.random.uniform(first, (GROUPS, rows, 1), minval=0.0, maxval=spread))
    column_scale = jnp.tile(jnp.exp(jax.random.uniform(second, (head_dim,), minval=0.0, maxval=spread)), width // head_dim)
    base = jax.random.normal(third, (GROUPS, rows, width))
    return base * row_scale * column_scale


def lengths_and_slots(key):

    def one_group(group_key):
        first, second, third = jax.random.split(group_key, 3)
        devices = RESPONSES // PER_DEV
        placed = jax.random.permutation(first, RESPONSES) % devices
        spans = jax.random.randint(second, (RESPONSES,), max(MOST // 4, 1), MOST + 1)
        full_device = jax.random.randint(third, (), 0, devices)
        spans = jnp.where(placed == full_device, MOST, spans)
        return (spans.astype(jnp.int32), placed.astype(jnp.int32))
    return jax.vmap(one_group)(jax.random.split(key, GROUPS))


def draw_lengths(key, part):
    return lengths_and_slots(key)[0]


def draw_assign(key, part):
    return lengths_and_slots(key)[1]


def draw_queries(key, part):
    key = jax.random.fold_in(key, 11)
    result = scaled_rows(key, SLOTS, QW, HEAD_DIM, math.log(10.0))
    return result.astype(jnp.bfloat16)


def draw_keys(key, part):
    key = jax.random.fold_in(key, 12)
    result = scaled_rows(key, SLOTS, KVW, HEAD_DIM, math.log(10.0))
    return result.astype(jnp.bfloat16)


def draw_prefix_keys(key, part):
    key = jax.random.fold_in(key, 13)
    first = jax.random.fold_in(key, 0)
    base = jax.random.normal(first, (GROUPS, PREFIX, KVW))
    result = base
    return result.astype(jnp.bfloat16)


def steps_of(rng, extent, cuts, least, high):
    def one(position, parts):
        heights = jax.random.uniform(jax.random.fold_in(jax.random.fold_in(rng, 6), position), (parts,), jnp.float32, least / len(cuts), high / len(cuts))
        return jnp.repeat(jnp.exp(heights), extent[position] // parts).reshape((-1,) + (1,) * (len(extent) - position - 1))

    level = one(*cuts[0])
    for cut in cuts[1:]:
        level = level * one(*cut)
    return level


def normal_values(stream_key, extent, scale, reach, cuts=(), kind=jnp.bfloat16):
    entries = jax.random.normal(stream_key, extent, jnp.float32) * scale
    if len(cuts) > 0:
        entries = steps_of(stream_key, extent, cuts, -0.22, 0.18) * entries
    return jnp.clip(entries, min=-reach, max=reach).astype(kind)


def setup_inputs(seed: int = 0) -> dict:
    splits = jax.random.split(jax.random.key(seed), 11)
    queries = draw_queries(jax.random.fold_in(splits[10], 71), 0)
    keys = draw_keys(jax.random.fold_in(splits[10], 71), 0)
    values = normal_values(splits[2], (GROUPS, SLOTS, KVW), 1.0, 6.0, ((0, 8), (1, 16)))
    prefix_keys = draw_prefix_keys(jax.random.fold_in(splits[10], 71), 0)
    prefix_values = normal_values(splits[4], (GROUPS, PREFIX, KVW), 1.0, 6.0, ((0, 8), (1, 16)))
    out_grad = normal_values(splits[5], (GROUPS, SLOTS, QW), 1.0, 6.0, ((0, 8), (1, 16)))
    q_gain = jnp.clip(1.0 + 0.15 * jax.random.normal(splits[6], (HEAD_DIM,), jnp.float32), 0.25, 1.75)
    k_gain = jnp.clip(1.0 + 0.15 * jax.random.normal(splits[7], (HEAD_DIM,), jnp.float32), 0.25, 1.75)
    lengths = draw_lengths(jax.random.fold_in(splits[10], 71), 0)
    assign = draw_assign(jax.random.fold_in(splits[10], 71), 0)
    return {"queries": queries, "keys": keys, "values": values, "prefix_keys": prefix_keys, "prefix_values": prefix_values, "out_grad": out_grad, "q_gain": q_gain, "k_gain": k_gain, "lengths": lengths, "assign": assign}


THETA = 1000000.0
EPS = 1e-06
MASKED = -1e+30

def rotary(values_in, positions):
    width = values_in.shape[-1]
    half = width // 2
    inverse = THETA ** (-(jnp.arange(half, dtype=jnp.float32) * 2.0 / width))
    angles = positions[:, None] * inverse[None, :]
    cosine = jnp.cos(angles)[:, None, :]
    sine = jnp.sin(angles)[:, None, :]
    lower = values_in[..., :half]
    upper = values_in[..., half:]
    return jnp.concatenate([lower * cosine - upper * sine, upper * cosine + lower * sine], axis=-1)

def prepare(raw, gain, positions):
    rows = raw.shape[0]
    head_dim = gain.shape[0]
    shaped = raw.reshape(rows, raw.shape[1] // head_dim, head_dim)
    normed = shaped * lax.rsqrt(lax.optimization_barrier(jnp.mean(shaped * shaped, axis=-1, keepdims=True)) + EPS) * gain
    return rotary(normed, positions).reshape(rows, raw.shape[1])

def layout(lengths_row, assign_row, device, slots):
    mine = assign_row == device
    spans = jnp.where(mine, lengths_row, 0).astype(jnp.int32)
    starts = (jnp.cumsum(spans) - spans).astype(jnp.int32)
    slot_ids = jnp.arange(slots, dtype=jnp.int32)
    inside = mine[None, :] & (slot_ids[:, None] >= starts[None, :]) & (slot_ids[:, None] < (starts + spans)[None, :])
    live = jnp.any(inside, axis=1)
    offsets = lax.optimization_barrier(jnp.sum(jnp.where(inside, slot_ids[:, None] - starts[None, :], 0), axis=1)).astype(jnp.int32)
    number = jnp.arange(lengths_row.shape[0], dtype=jnp.int32)
    owners = lax.optimization_barrier(jnp.sum(jnp.where(inside, number[None, :], 0), axis=1)).astype(jnp.int32)
    self_mask = live[:, None] & live[None, :] & (owners[:, None] == owners[None, :]) & (slot_ids[None, :] <= slot_ids[:, None])
    return (live, offsets, self_mask)

def device_pass(query_raw, key_raw, value_raw, grad_out, prefix_k, prefix_v, q_gain, k_gain, lengths_row, assign_row, device):
    slots = query_raw.shape[0]
    head_dim = q_gain.shape[0]
    prefix = prefix_k.shape[0]
    kv_heads = key_raw.shape[1] // head_dim
    grouped = query_raw.shape[1] // key_raw.shape[1]
    live, offsets, self_mask = layout(lengths_row, assign_row, device, slots)
    positions = (prefix + offsets).astype(jnp.float32)
    q_float = query_raw.astype(jnp.float32)
    k_float = key_raw.astype(jnp.float32)
    query_n = prepare(q_float, q_gain, positions).astype(jnp.bfloat16)
    key_n = prepare(k_float, k_gain, positions).astype(jnp.bfloat16)
    all_keys = jnp.concatenate([prefix_k, key_n], axis=0).reshape(prefix + slots, kv_heads, head_dim)
    all_values = jnp.concatenate([prefix_v, value_raw], axis=0).reshape(prefix + slots, kv_heads, head_dim)
    mask = jnp.concatenate([jnp.ones((slots, prefix), dtype=bool), self_mask], axis=1)
    query_four = query_n.reshape(slots, kv_heads, grouped, head_dim)
    grad_live = jnp.where(live[:, None], grad_out, jnp.zeros_like(grad_out))
    grad_float = grad_live.astype(jnp.float32).reshape(slots, kv_heads, grouped, head_dim)
    scale = head_dim ** (-0.5)
    scores = jnp.einsum('qhgd,khd->hgqk', query_four.astype(jnp.float32), all_keys.astype(jnp.float32)) * scale
    scores = jnp.where(mask[None, None], scores, MASKED)
    highest = lax.optimization_barrier(jnp.max(scores, axis=-1, keepdims=True))
    expd = jnp.exp(scores - highest)
    weights = expd / lax.optimization_barrier(jnp.sum(expd, axis=-1, keepdims=True))
    weights_b = weights.astype(jnp.bfloat16)
    output = jnp.einsum('hgqk,khd->qhgd', weights_b.astype(jnp.float32), all_values.astype(jnp.float32))
    output = jnp.where(live[:, None, None, None], output, 0.0).astype(jnp.bfloat16)
    dprob = jnp.einsum('qhgd,khd->hgqk', grad_float, all_values.astype(jnp.float32))
    rowdot = jnp.einsum('qhgd,qhgd->hgq', grad_float, output.astype(jnp.float32))
    dscore = (weights * (dprob - rowdot[..., None]) * scale).astype(jnp.bfloat16)
    grad_qn = jnp.einsum('hgqk,khd->qhgd', dscore.astype(jnp.float32), all_keys.astype(jnp.float32)).reshape(slots, -1)
    grad_kn = jnp.einsum('hgqk,qhgd->khd', dscore.astype(jnp.float32), query_four.astype(jnp.float32)).reshape(prefix + slots, -1)
    grad_vn = jnp.einsum('hgqk,qhgd->khd', weights_b.astype(jnp.float32), grad_float).reshape(prefix + slots, -1)
    _, pull_query = jax.vjp(lambda raw, gain: prepare(raw, gain, positions), q_float, q_gain)
    grad_query, grad_qgain = pull_query(grad_qn)
    _, pull_key = jax.vjp(lambda raw, gain: prepare(raw, gain, positions), k_float, k_gain)
    grad_key, grad_kgain = pull_key(grad_kn[prefix:])
    return (output.reshape(slots, -1), grad_query.astype(jnp.bfloat16), grad_key.astype(jnp.bfloat16), grad_vn[prefix:].astype(jnp.bfloat16), grad_kn[:prefix], grad_vn[:prefix], grad_qgain, grad_kgain)

def reference(queries, keys, values, prefix_keys, prefix_values, out_grad, q_gain, k_gain, lengths, assign):
    groups, total, qwidth = queries.shape
    slots = total // N_RESP
    prefix = prefix_keys.shape[1]
    kv_width = keys.shape[2]
    head_dim = q_gain.shape[0]

    def one_group(index):

        def one_device(carry, device):
            start = device * slots
            pieces = [lax.dynamic_slice_in_dim(array[index], start, slots, 0) for array in (queries, keys, values, out_grad)]
            result = device_pass(pieces[0], pieces[1], pieces[2], pieces[3], prefix_keys[index], prefix_values[index], q_gain, k_gain, lengths[index], assign[index], device)
            carry = tuple((older + newer for older, newer in zip(carry, result[4:])))
            return (carry, result[:4])
        start_sums = (jnp.zeros((prefix, kv_width), jnp.float32), jnp.zeros((prefix, kv_width), jnp.float32), jnp.zeros((head_dim,), jnp.float32), jnp.zeros((head_dim,), jnp.float32))
        return lax.scan(one_device, start_sums, jnp.arange(N_RESP, dtype=jnp.int32))
    sums, stacked = lax.map(one_group, jnp.arange(groups, dtype=jnp.int32))
    attention = stacked[0].reshape(groups, total, qwidth)
    grad_queries = stacked[1].reshape(groups, total, qwidth)
    grad_keys = stacked[2].reshape(groups, total, kv_width)
    grad_values = stacked[3].reshape(groups, total, kv_width)
    return (attention, grad_queries, grad_keys, grad_values, sums[0].astype(jnp.bfloat16), sums[1].astype(jnp.bfloat16), lax.optimization_barrier(jnp.sum(sums[2], axis=0)), lax.optimization_barrier(jnp.sum(sums[3], axis=0)))
```

```python
import functools
import math

import jax
import jax.numpy as jnp
import numpy as np
from jax import lax
from jax.experimental import pallas as pl
from jax.experimental.pallas import tpu as pltpu
from jax.sharding import PartitionSpec as P

THETA = 1000000.0
EPS = 1e-06
MASKED = -1e30
D = 128
NT = (((1,), (1,)), ((), ()))
NN = (((1,), (0,)), ((), ()))
CHUNKS = 1


def dot(a, b, dims):
    return lax.dot_general(a, b, dims, preferred_element_type=jnp.float32)


def tables(slots, prefix):
    half = D // 2
    inverse = (THETA ** (-(np.arange(half, dtype=np.float32) * np.float32(2.0 / D)))).astype(np.float32)
    positions = (prefix + np.arange(slots)).astype(np.float32)
    angles = (positions[:, None] * inverse[None, :]).astype(np.float64)
    cosine, sine = np.cos(angles), np.sin(angles)
    return (
        np.concatenate([cosine, cosine], axis=1).astype(np.float32),
        np.concatenate([-sine, sine], axis=1).astype(np.float32),
    )


def swap(x):
    return pltpu.roll(x, D // 2, 1)


def norm_rope(raw, gain, cosine, sine):
    x = raw.astype(jnp.float32)
    inv = lax.rsqrt(jnp.mean(x * x, axis=1, keepdims=True) + EPS)
    hat = x * inv
    scaled = hat * gain
    return (scaled * cosine + swap(scaled) * sine).astype(jnp.bfloat16), hat, inv


def norm_rope_back(grad, hat, inv, gain, cosine, sine):
    back = grad * cosine - swap(grad) * sine
    by_hat = back * hat
    mean = jnp.mean(by_hat * gain, axis=1, keepdims=True)
    return inv * (back * gain - hat * mean), by_hat


def fold_rows(x):
    total = x[0:8]
    for start in range(8, x.shape[0], 8):
        total = total + x[start : start + 8]
    return total


def kernel(
    len_ref, q_ref, og_ref, k_ref, v_ref, ak_ref, av_ref, bk_ref, bv_ref, cos_ref, sin_ref, qg_ref, kg_ref,
    *rest,
    grouped, carried,
):
    rest = rest[carried:]
    (out_ref, gq_ref, gk_ref, gv_ref, dak_ref, dav_ref, dbk_ref, dbv_ref, gain_ref,
     keys, vals, keys_t, vals_t, probs, dscores) = rest
    slots = q_ref.shape[0]
    part = ak_ref.shape[0]
    prefix = 2 * part
    total = prefix + slots
    scale = D ** (-0.5)
    log_scale = scale * math.log2(math.e)
    bf = jnp.bfloat16
    cosine, sine = cos_ref[...], sin_ref[...]
    q_gain, k_gain = qg_ref[...], kg_ref[...]

    @pl.when(pl.program_id(0) == 0)
    def _():
        gain_ref[...] = jnp.zeros_like(gain_ref)

    key_n, key_hat, key_inv = norm_rope(k_ref[...], k_gain, cosine, sine)
    keys[0:part, :] = ak_ref[...]
    keys[part:prefix, :] = bk_ref[...]
    keys[prefix:total, :] = key_n
    vals[0:part, 0:D] = av_ref[...]
    vals[part:prefix, 0:D] = bv_ref[...]
    vals[prefix:total, 0:D] = v_ref[...]
    vals[:, D : 2 * D] = jnp.ones((total, D), bf)
    keys_t[...] = keys[...].T
    vals_t[...] = vals[:, 0:D].T

    length = len_ref[0]
    live = lax.broadcasted_iota(jnp.int32, (slots, 1), 0) < length
    live2 = jnp.concatenate([live, live], axis=0)
    row = lax.broadcasted_iota(jnp.int32, (slots, 2 * slots), 0)
    col = lax.broadcasted_iota(jnp.int32, (slots, 2 * slots), 1)
    causal = row <= jnp.where(col >= slots, col - slots, col)
    lane = lax.broadcasted_iota(jnp.int32, (2 * slots, D), 1)
    gain_sum = jnp.zeros((8, D), jnp.float32)
    queries_n, grads = [], []
    for pair in range(grouped // 2):
        cols = [slice((2 * pair + j) * D, (2 * pair + j + 1) * D) for j in range(2)]
        prepared = [norm_rope(q_ref[:, c], q_gain, cosine, sine) for c in cols]
        query = jnp.concatenate([p[0] for p in prepared], axis=0)
        grad_f = jnp.where(
            live2, jnp.concatenate([og_ref[:, c] for c in cols], axis=0).astype(jnp.float32), 0.0
        )
        grad = grad_f.astype(bf)
        queries_n.append(query)
        grads.append(grad)
        scores = dot(keys[...], query, NT)
        own = jnp.where(causal, scores[prefix:], MASKED)
        scores = jnp.concatenate([scores[:prefix], own], axis=0)
        highest = jnp.max(scores, axis=0, keepdims=True)
        expd = jnp.exp2((scores - highest) * log_scale)
        weights = expd * (1.0 / jnp.sum(expd, axis=0, keepdims=True))
        weights_b = weights.astype(bf)
        here = slice(pair * 2 * slots, (pair + 1) * 2 * slots)
        probs[:, here] = weights_b
        output = dot(vals_t[...], weights_b, NN).T
        output = jnp.where(live2, output, 0.0).astype(bf)
        for j in range(2):
            out_ref[:, cols[j]] = output[j * slots : (j + 1) * slots]
        product = grad_f * output.astype(jnp.float32)
        product = product + swap(product)
        high = product.astype(bf).astype(jnp.float32)
        rowdot = jnp.where(lane < D // 2, high, product - high)
        augmented = jnp.concatenate([grad, (-rowdot).astype(bf)], axis=1)
        dprob = dot(vals[...], augmented, NT)
        dscore = (weights * dprob * scale).astype(bf)
        dscores[:, here] = dscore
        grad_qn = dot(keys_t[...], dscore, NN).T
        for j in range(2):
            back, by_hat = norm_rope_back(
                grad_qn[j * slots : (j + 1) * slots], prepared[j][1], prepared[j][2], q_gain, cosine, sine
            )
            gq_ref[:, cols[j]] = back.astype(bf)
            gain_sum = gain_sum + fold_rows(by_hat)
    grad_kn = dot(dscores[...], jnp.concatenate(queries_n, axis=0), NN)
    grad_vn = dot(probs[...], jnp.concatenate(grads, axis=0), NN)
    dak_ref[...] = grad_kn[:part].astype(dak_ref.dtype)
    dbk_ref[...] = grad_kn[part:prefix].astype(dbk_ref.dtype)
    dav_ref[...] = grad_vn[:part].astype(dav_ref.dtype)
    dbv_ref[...] = grad_vn[part:prefix].astype(dbv_ref.dtype)
    gv_ref[...] = grad_vn[prefix:].astype(bf)
    back, by_hat = norm_rope_back(grad_kn[prefix:], key_hat, key_inv, k_gain, cosine, sine)
    gk_ref[...] = back.astype(bf)
    gain_ref[0:8, :] += gain_sum
    gain_ref[8:16, :] += fold_rows(by_hat)


def attend(first, heads, length, queries, out_grad, keys, values, part_a, part_b, cosine, sine, q_gain, k_gain, carry):
    slots, width = queries.shape
    kv_width = keys.shape[1]
    grouped = width // kv_width
    part = part_a.shape[0]
    bf = jnp.bfloat16
    whole = lambda shape: pl.BlockSpec(shape, lambda i: (0, 0))
    wide = pl.BlockSpec((slots, grouped * D), lambda i: (0, first + i))
    thin = pl.BlockSpec((slots, D), lambda i: (0, first + i))
    lead = pl.BlockSpec((part, D), lambda i: (0, i))
    second = pl.BlockSpec((part, D), lambda i: (0, heads + i))
    total = 2 * part + slots
    carried = [] if carry is None else list(carry)
    outs = [
        jax.ShapeDtypeStruct((slots, width), bf),
        jax.ShapeDtypeStruct((slots, width), bf),
        jax.ShapeDtypeStruct((slots, kv_width), bf),
        jax.ShapeDtypeStruct((slots, kv_width), bf),
        jax.ShapeDtypeStruct((part, heads * D), jnp.float32),
        jax.ShapeDtypeStruct((part, heads * D), jnp.float32),
        jax.ShapeDtypeStruct((part, heads * D), bf),
        jax.ShapeDtypeStruct((part, heads * D), bf),
        jax.ShapeDtypeStruct((16, D), jnp.float32),
    ]
    flops = 6 * 2 * heads * grouped * slots * D * total
    return pl.pallas_call(
        functools.partial(kernel, grouped=grouped, carried=len(carried)),
        grid=(heads,),
        out_shape=outs,
        in_specs=[
            pl.BlockSpec(memory_space=pltpu.SMEM),
            wide, wide, thin, thin, lead, second, lead, second,
            whole((slots, D)), whole((slots, D)), whole((1, D)), whole((1, D)),
        ] + [pl.BlockSpec(memory_space=pl.ANY)] * len(carried),
        out_specs=[wide, wide, thin, thin, lead, lead, lead, lead, whole((16, D))],
        scratch_shapes=[
            pltpu.VMEM((total, D), bf),
            pltpu.VMEM((total, 2 * D), bf),
            pltpu.VMEM((D, total), bf),
            pltpu.VMEM((D, total), bf),
            pltpu.VMEM((total, grouped * slots), bf),
            pltpu.VMEM((total, grouped * slots), bf),
        ],
        input_output_aliases={13 + n: n for n in range(len(carried))},
        compiler_params=pltpu.CompilerParams(
            dimension_semantics=("arbitrary",), vmem_limit_bytes=40 * 1024 * 1024
        ),
        cost_estimate=pl.CostEstimate(
            flops=2 * flops, bytes_accessed=heads * grouped * slots * D * 8, transcendentals=heads * grouped * slots * total
        ),
        name="attend",
    )(length, queries, out_grad, keys, values, part_a, part_a, part_b, part_b, cosine, sine, q_gain, k_gain, *carried)


def exchange(x, mask, count):
    return lax.ppermute(x, "resp", [(i, i ^ mask) for i in range(count)])


def shards(
    queries, keys, values, prefix_keys, prefix_values, out_grad, q_gain, k_gain, lengths, assign
):
    slots = queries.shape[1]
    kv_heads = keys.shape[2] // D
    count = lax.axis_size("resp")
    rows = prefix_keys.shape[1]
    peers = count // 2
    device = lax.axis_index("resp")
    length = jnp.sum(jnp.where(assign[0] == device, lengths[0], 0)).reshape(1)
    cosine, sine = (jnp.asarray(t) for t in tables(slots, rows * count))
    heads = kv_heads // CHUNKS
    width = heads * D
    f32, bf = jnp.float32, jnp.bfloat16

    gathered = []
    for c in range(CHUNKS):
        cols = slice(c * width, (c + 1) * width)
        mine = jnp.concatenate([prefix_keys[0, :, cols], prefix_values[0, :, cols]], axis=1)
        part_a = jnp.concatenate([mine] + [exchange(mine, 2 * s, count) for s in range(1, peers)], axis=0)
        gathered.append((part_a, exchange(part_a, 1, count)))

    carry = None
    gains = jnp.zeros((16, D), f32)
    pkeys, pvalues = [], []
    for c in range(CHUNKS):
        results = attend(
            c * heads, heads, length, queries[0], out_grad[0], keys[0], values[0], *gathered[c],
            cosine, sine, q_gain.reshape(1, D), k_gain.reshape(1, D), carry,
        )
        carry = results[:4]
        dak, dav, dbk, dbv = results[4:8]
        gains = gains + results[8]
        other = exchange(jnp.concatenate([dbk, dbv], axis=1), 1, count).astype(f32)
        sums = jnp.concatenate([dak, dav], axis=1) + other
        sums_b = sums.astype(bf)
        owned = sums[:rows]
        for s in range(1, peers):
            owned = owned + exchange(sums_b[s * rows : (s + 1) * rows], 2 * s, count).astype(f32)
        owned = owned.astype(bf)
        pkeys.append(owned[:, :width])
        pvalues.append(owned[:, width:])

    gains = jnp.sum(gains.reshape(2, 8, D), axis=1).reshape(1, 2 * D)
    devices = count * lax.axis_size("prompt")
    spread = lax.all_to_all(jnp.broadcast_to(gains, (devices, 2 * D)), ("prompt", "resp"), 0, 0)
    gains = jnp.sum(spread.reshape(devices, 2 * D), axis=0)
    attention, grad_q, grad_k, grad_v = carry
    return (
        attention[None],
        grad_q[None],
        grad_k[None],
        grad_v[None],
        jnp.concatenate(pkeys, axis=1)[None],
        jnp.concatenate(pvalues, axis=1)[None],
        gains[:D],
        gains[D:],
    )


def solution(mesh):
    rows = P("prompt", "resp", None)
    groups = P("prompt", None)
    return jax.shard_map(
        shards,
        mesh=mesh,
        in_specs=(rows, rows, rows, rows, rows, rows, P(), P(), groups, groups),
        out_specs=(rows, rows, rows, rows, rows, rows, P(), P()),
        check_vma=False,
    )
```

```python
import functools
import math

import jax
import jax.numpy as jnp
import numpy as np
from jax import lax
from jax.experimental import pallas as pl
from jax.experimental.pallas import tpu as pltpu
from jax.sharding import PartitionSpec as P

THETA = 1000000.0
EPS = 1e-06
MASKED = -1e30
D = 128
NT = (((1,), (1,)), ((), ()))
NN = (((1,), (0,)), ((), ()))
CHUNKS = 1
PER = 2
BLOCK = 64
DOT = 640


def dot(a, b, dims):
    return lax.dot_general(a, b, dims, preferred_element_type=jnp.float32)


def tables(slots, prefix):
    half = D // 2
    inverse = (THETA ** (-(np.arange(half, dtype=np.float32) * np.float32(2.0 / D)))).astype(np.float32)
    positions = (prefix + np.arange(slots)).astype(np.float32)
    angles = (positions[:, None] * inverse[None, :]).astype(np.float64)
    cosine, sine = np.cos(angles), np.sin(angles)
    return (
        np.concatenate([cosine, cosine], axis=1).astype(np.float32),
        np.concatenate([-sine, sine], axis=1).astype(np.float32),
    )


def swap(x):
    return pltpu.roll(x, D // 2, 1)


def norm_rope(raw, gain, cosine, sine):
    x = raw.astype(jnp.float32)
    inv = lax.rsqrt(jnp.mean(x * x, axis=1, keepdims=True) + EPS)
    hat = x * inv
    scaled = hat * gain
    return (scaled * cosine + swap(scaled) * sine).astype(jnp.bfloat16), hat, inv


def norm_rope_back(grad, hat, inv, gain, cosine, sine):
    back = grad * cosine - swap(grad) * sine
    by_hat = back * hat
    mean = jnp.mean(by_hat * gain, axis=1, keepdims=True)
    return inv * (back * gain - hat * mean), by_hat


def fold_rows(x):
    total = x[0:8]
    for start in range(8, x.shape[0], 8):
        total = total + x[start : start + 8]
    return total


def fold_max(x):
    total = x[0:8]
    for start in range(8, x.shape[0], 8):
        total = jnp.maximum(total, x[start : start + 8])
    return total


def kernel(
    len_ref, q_ref, og_ref, k_ref, v_ref, ak_ref, av_ref, bk_ref, bv_ref, cos_ref, sin_ref, qg_ref, kg_ref,
    *rest,
    grouped, carried,
):
    rest = rest[carried:]
    (out_ref, gq_ref, gk_ref, gv_ref, dak_ref, dav_ref, dbk_ref, dbv_ref, gain_ref,
     keys, vals, keys_t, vals_t, scores, dprobs, probs, dscores, acc_k, acc_v) = rest
    slots = q_ref.shape[0]
    part = ak_ref.shape[0]
    prefix = 2 * part
    total = prefix + slots
    scale = D ** (-0.5)
    log_scale = scale * math.log2(math.e)
    bf = jnp.bfloat16
    cosine, sine = cos_ref[...], sin_ref[...]
    q_gain, k_gain = qg_ref[...], kg_ref[...]
    pairs = grouped // 2
    width = 2 * slots
    blocks = [slice(r, r + BLOCK) for r in range(0, total, BLOCK)]

    @pl.when(pl.program_id(0) == 0)
    def _():
        gain_ref[...] = jnp.zeros_like(gain_ref)

    per = k_ref.shape[1] // D
    kept = []
    for h in range(per):
        here_h = slice(h * D, (h + 1) * D)
        key_n, key_hat, key_inv = norm_rope(k_ref[:, here_h], k_gain, cosine, sine)
        kept.append((key_hat, key_inv))
        keys[h, 0:part, :] = ak_ref[:, here_h]
        keys[h, part:prefix, :] = bk_ref[:, here_h]
        keys[h, prefix:total, :] = key_n
        vals[h, 0:part, :] = av_ref[:, here_h]
        vals[h, part:prefix, :] = bv_ref[:, here_h]
        vals[h, prefix:total, :] = v_ref[:, here_h]
        keys_t[h] = keys[h].T
        vals_t[h] = vals[h].T

    length = len_ref[0]
    live = lax.broadcasted_iota(jnp.int32, (slots, 1), 0) < length
    col1 = lax.broadcasted_iota(jnp.int32, (1, width), 1)
    slot1 = jnp.where(col1 >= slots, col1 - slots, col1)
    live_t = slot1 < length
    cols = lambda p: [slice((2 * p + j) * D, (2 * p + j + 1) * D) for j in range(2)]
    here = lambda p: slice((p % 2) * width, (p % 2 + 1) * width)
    state = [dict() for _ in range(per * pairs)]
    head = lambda p: p // pairs

    def prepare(p):
        st = state[p]
        st["prep"] = [norm_rope(q_ref[:, c], q_gain, cosine, sine) for c in cols(p)]
        st["query"] = jnp.concatenate([x[0] for x in st["prep"]], axis=0)
        grad = [jnp.where(live, og_ref[:, c].astype(jnp.float32), 0.0).astype(bf) for c in cols(p)]
        st["grad"] = jnp.concatenate(grad, axis=0)
        st["grad_t"] = st["grad"].T

    def multiply_in(p):
        st = state[p]
        top = jnp.full((8, width), MASKED, jnp.float32)
        for start in range(0, total, DOT):
            big = dot(keys[head(p), start : start + DOT, :], st["query"], NT)
            for off in range(0, DOT, BLOCK):
                rows = slice(start + off, start + off + BLOCK)
                s = big[off : off + BLOCK]
                if rows.start >= prefix:
                    row = lax.broadcasted_iota(jnp.int32, (BLOCK, width), 0) + (rows.start - prefix)
                    s = jnp.where(row <= slot1, s, MASKED)
                scores[p % 2, rows, :] = s
                top = jnp.maximum(top, fold_max(s))
        st["top"] = top
        for start in range(0, total, DOT):
            rows = slice(start, start + DOT)
            dprobs[p % 2, rows, :] = dot(vals[head(p), rows, :], st["grad"], NT)

    def soften(p):
        st = state[p]
        top = jnp.max(st["top"], axis=0, keepdims=True) * log_scale
        mass = jnp.zeros((8, width), jnp.float32)
        for rows in blocks:
            e = jnp.exp2(scores[p % 2, rows, :] * log_scale - top)
            scores[p % 2, rows, :] = e
            mass = mass + fold_rows(e)
        st["inv"] = 1.0 / jnp.sum(mass, axis=0, keepdims=True)
        for rows in blocks:
            probs[rows, here(p)] = (scores[p % 2, rows, :] * st["inv"]).astype(bf)

    def multiply_out(p):
        st = state[p]
        output = dot(vals_t[head(p)], probs[:, here(p)], NN)
        output = jnp.where(live_t, output, 0.0).astype(bf)
        st["rowdot"] = jnp.sum(output.astype(jnp.float32) * st["grad_t"].astype(jnp.float32), axis=0, keepdims=True)
        turned = output.T
        for j in range(2):
            out_ref[:, cols(p)[j]] = turned[j * slots : (j + 1) * slots]

    def value_grad(p):
        more = dot(probs[:, here(p)], state[p]["grad"], NN)
        acc_v[head(p)] = more if p % pairs == 0 else acc_v[head(p)] + more

    def score_grad(p):
        st = state[p]
        inv = st["inv"] * scale
        for rows in blocks:
            dscores[rows, here(p)] = (
                (scores[p % 2, rows, :] * inv) * (dprobs[p % 2, rows, :] - st["rowdot"])
            ).astype(bf)

    def query_key_grad(p):
        st = state[p]
        st["grad_qn"] = dot(keys_t[head(p)], dscores[:, here(p)], NN).T
        more = dot(dscores[:, here(p)], st["query"], NN)
        acc_k[head(p)] = more if p % pairs == 0 else acc_k[head(p)] + more

    def query_back(p):
        st = state[p]
        total_gain = jnp.zeros((8, D), jnp.float32)
        for j in range(2):
            back, by_hat = norm_rope_back(
                st["grad_qn"][j * slots : (j + 1) * slots], st["prep"][j][1], st["prep"][j][2], q_gain, cosine, sine
            )
            gq_ref[:, cols(p)[j]] = back.astype(bf)
            total_gain = total_gain + fold_rows(by_hat)
        gain_ref[0:8, :] += total_gain

    def finish(h):
        here_h = slice(h * D, (h + 1) * D)
        grad_kn, grad_vn = acc_k[h], acc_v[h]
        dak_ref[:, here_h] = grad_kn[:part].astype(dak_ref.dtype)
        dbk_ref[:, here_h] = grad_kn[part:prefix].astype(dbk_ref.dtype)
        dav_ref[:, here_h] = grad_vn[:part].astype(dav_ref.dtype)
        dbv_ref[:, here_h] = grad_vn[part:prefix].astype(dbv_ref.dtype)
        gv_ref[:, here_h] = grad_vn[prefix:].astype(bf)
        back, by_hat = norm_rope_back(grad_kn[prefix:], kept[h][0], kept[h][1], k_gain, cosine, sine)
        gk_ref[:, here_h] = back.astype(bf)
        gain_ref[8:16, :] += fold_rows(by_hat)

    count = per * pairs
    prepare(0)
    multiply_in(0)
    for p in range(count):
        if p + 1 < count:
            prepare(p + 1)
        soften(p)
        if p + 1 < count:
            multiply_in(p + 1)
        if p > 0:
            query_key_grad(p - 1)
        multiply_out(p)
        value_grad(p)
        if p > 0:
            query_back(p - 1)
            if p % pairs == 0:
                finish(head(p - 1))
        score_grad(p)
    query_key_grad(count - 1)
    query_back(count - 1)
    finish(per - 1)


def attend(first, heads, length, queries, out_grad, keys, values, part_a, part_b, cosine, sine, q_gain, k_gain, carry):
    slots, width = queries.shape
    kv_width = keys.shape[1]
    grouped = width // kv_width
    part = part_a.shape[0]
    bf = jnp.bfloat16
    steps, start = heads // PER, first // PER
    whole = lambda shape: pl.BlockSpec(shape, lambda i: (0, 0))
    wide = pl.BlockSpec((slots, PER * grouped * D), lambda i: (0, start + i))
    thin = pl.BlockSpec((slots, PER * D), lambda i: (0, start + i))
    lead = pl.BlockSpec((part, PER * D), lambda i: (0, i))
    second = pl.BlockSpec((part, PER * D), lambda i: (0, steps + i))
    total = 2 * part + slots
    carried = [] if carry is None else list(carry)
    outs = [
        jax.ShapeDtypeStruct((slots, width), bf),
        jax.ShapeDtypeStruct((slots, width), bf),
        jax.ShapeDtypeStruct((slots, kv_width), bf),
        jax.ShapeDtypeStruct((slots, kv_width), bf),
        jax.ShapeDtypeStruct((part, heads * D), jnp.float32),
        jax.ShapeDtypeStruct((part, heads * D), jnp.float32),
        jax.ShapeDtypeStruct((part, heads * D), bf),
        jax.ShapeDtypeStruct((part, heads * D), bf),
        jax.ShapeDtypeStruct((16, D), jnp.float32),
    ]
    flops = 6 * 2 * heads * grouped * slots * D * total
    return pl.pallas_call(
        functools.partial(kernel, grouped=grouped, carried=len(carried)),
        grid=(steps,),
        out_shape=outs,
        in_specs=[
            pl.BlockSpec(memory_space=pltpu.SMEM),
            wide, wide, thin, thin, lead, second, lead, second,
            whole((slots, D)), whole((slots, D)), whole((1, D)), whole((1, D)),
        ] + [pl.BlockSpec(memory_space=pl.ANY)] * len(carried),
        out_specs=[wide, wide, thin, thin, lead, lead, lead, lead, whole((16, D))],
        scratch_shapes=[
            pltpu.VMEM((PER, total, D), bf),
            pltpu.VMEM((PER, total, D), bf),
            pltpu.VMEM((PER, D, total), bf),
            pltpu.VMEM((PER, D, total), bf),
            pltpu.VMEM((2, total, 2 * slots), jnp.float32),
            pltpu.VMEM((2, total, 2 * slots), jnp.float32),
            pltpu.VMEM((total, 4 * slots), bf),
            pltpu.VMEM((total, 4 * slots), bf),
            pltpu.VMEM((PER, total, D), jnp.float32),
            pltpu.VMEM((PER, total, D), jnp.float32),
        ],
        input_output_aliases={13 + n: n for n in range(len(carried))},
        compiler_params=pltpu.CompilerParams(
            dimension_semantics=("arbitrary",), vmem_limit_bytes=40 * 1024 * 1024
        ),
        cost_estimate=pl.CostEstimate(
            flops=2 * flops, bytes_accessed=heads * grouped * slots * D * 8, transcendentals=heads * grouped * slots * total
        ),
        name="attend",
    )(length, queries, out_grad, keys, values, part_a, part_a, part_b, part_b, cosine, sine, q_gain, k_gain, *carried)


def moved(x, count, dz=0, dy=0, dc=0):
    ring = count // 4

    def target(i):
        z, y, c = i // (2 * ring), i // 2 % ring, i % 2
        return (z + dz) % 2 * 2 * ring + (y + dy) % ring * 2 + (c + dc) % 2

    return lax.ppermute(x, "resp", [(i, target(i)) for i in range(count)])


def shards(
    queries, keys, values, prefix_keys, prefix_values, out_grad, q_gain, k_gain, lengths, assign
):
    slots = queries.shape[1]
    kv_heads = keys.shape[2] // D
    count = lax.axis_size("resp")
    rows = prefix_keys.shape[1]
    ring = count // 4
    device = lax.axis_index("resp")
    length = jnp.sum(jnp.where(assign[0] == device, lengths[0], 0)).reshape(1)
    cosine, sine = (jnp.asarray(t) for t in tables(slots, rows * count))
    heads = kv_heads // CHUNKS
    width = heads * D
    f32, bf = jnp.float32, jnp.bfloat16

    gathered = []
    for c in range(CHUNKS):
        cols = slice(c * width, (c + 1) * width)
        mine = jnp.concatenate([prefix_keys[0, :, cols], prefix_values[0, :, cols]], axis=1)
        both = jnp.concatenate([mine, moved(mine, count, dz=1)], axis=0)
        pieces = [both] + [moved(both, count, dy=d) for d in range(1, ring)]
        others = [moved(piece, count, dc=1) for piece in pieces]
        gathered.append((jnp.concatenate(pieces, axis=0), jnp.concatenate(others, axis=0)))

    carry = None
    gains = jnp.zeros((16, D), f32)
    pkeys, pvalues = [], []
    for c in range(CHUNKS):
        results = attend(
            c * heads, heads, length, queries[0], out_grad[0], keys[0], values[0], *gathered[c],
            cosine, sine, q_gain.reshape(1, D), k_gain.reshape(1, D), carry,
        )
        carry = results[:4]
        dak, dav, dbk, dbv = results[4:8]
        gains = gains + results[8]
        other = moved(jnp.concatenate([dbk, dbv], axis=1), count, dc=1).astype(f32)
        sums = jnp.concatenate([dak, dav], axis=1) + other
        sums_b = sums.astype(bf)
        owned = sums[: 2 * rows]
        for d in range(1, ring):
            owned = owned + moved(sums_b[2 * d * rows : 2 * (d + 1) * rows], count, dy=ring - d).astype(f32)
        owned = owned[:rows] + moved(owned[rows:].astype(bf), count, dz=1).astype(f32)
        owned = owned.astype(bf)
        pkeys.append(owned[:, :width])
        pvalues.append(owned[:, width:])

    gains = jnp.sum(gains.reshape(2, 8, D), axis=1).reshape(1, 2 * D)
    devices = count * lax.axis_size("prompt")
    spread = lax.all_to_all(jnp.broadcast_to(gains, (devices, 2 * D)), ("prompt", "resp"), 0, 0)
    gains = jnp.sum(spread.reshape(devices, 2 * D), axis=0)
    attention, grad_q, grad_k, grad_v = carry
    return (
        attention[None],
        grad_q[None],
        grad_k[None],
        grad_v[None],
        jnp.concatenate(pkeys, axis=1)[None],
        jnp.concatenate(pvalues, axis=1)[None],
        gains[:D],
        gains[D:],
    )


def solution(mesh):
    rows = P("prompt", "resp", None)
    groups = P("prompt", None)
    return jax.shard_map(
        shards,
        mesh=mesh,
        in_specs=(rows, rows, rows, rows, rows, rows, P(), P(), groups, groups),
        out_specs=(rows, rows, rows, rows, rows, rows, P(), P()),
        check_vma=False,
    )
```

```python
import functools
import math

import jax
import jax.numpy as jnp
import numpy as np
from jax import lax
from jax.experimental import pallas as pl
from jax.experimental.pallas import tpu as pltpu
from jax.sharding import PartitionSpec as P

THETA = 1000000.0
EPS = 1e-06
MASKED = -1e30
D = 128
NT = (((1,), (1,)), ((), ()))
NN = (((1,), (0,)), ((), ()))
PER = 4
BLOCK = 64
DOT = 640


def dot(a, b, dims):
    return lax.dot_general(a, b, dims, preferred_element_type=jnp.float32)


def tables(slots, prefix):
    half = D // 2
    inverse = (THETA ** (-(np.arange(half, dtype=np.float32) * np.float32(2.0 / D)))).astype(np.float32)
    positions = (prefix + np.arange(slots)).astype(np.float32)
    angles = (positions[:, None] * inverse[None, :]).astype(np.float64)
    cosine, sine = np.cos(angles), np.sin(angles)
    return (
        np.concatenate([cosine, cosine], axis=1).astype(np.float32),
        np.concatenate([-sine, sine], axis=1).astype(np.float32),
    )


def swap(x):
    return pltpu.roll(x, D // 2, 1)


def norm_rope(raw, gain, cosine, sine):
    x = raw.astype(jnp.float32)
    inv = lax.rsqrt(jnp.mean(x * x, axis=1, keepdims=True) + EPS)
    hat = x * inv
    scaled = hat * gain
    return (scaled * cosine + swap(scaled) * sine).astype(jnp.bfloat16), hat, inv


def norm_rope_back(grad, hat, inv, gain, cosine, sine):
    back = grad * cosine - swap(grad) * sine
    by_hat = back * hat
    mean = jnp.mean(by_hat * gain, axis=1, keepdims=True)
    return inv * (back * gain - hat * mean), by_hat


def fold_rows(x):
    total = x[0:8]
    for start in range(8, x.shape[0], 8):
        total = total + x[start : start + 8]
    return total


def fold_max(x):
    total = x[0:8]
    for start in range(8, x.shape[0], 8):
        total = jnp.maximum(total, x[start : start + 8])
    return total


def kernel(
    lengths_ref, assign_ref, qg_ref, kg_ref, q_hbm, og_hbm, k_hbm, v_hbm, table_hbm,
    *rest,
    grouped, places,
):
    arrivals, rest = rest[: 2 * len(places)], rest[2 * len(places) :]
    (out_ref, gq_ref, gk_ref, gv_ref, da_ref, db_ref, gain_ref,
     keys, vals, keys_t, vals_t, scores, dprobs, probs, dscores, acc_k, acc_v,
     q_two, og_two, k_two, v_two, table, sems, table_sem) = rest
    step = pl.program_id(0)
    now = lax.rem(step, 2)

    def loads(index, slot):
        pairs_of = ((q_hbm, q_two), (og_hbm, og_two), (k_hbm, k_two), (v_hbm, v_two))
        return [
            pltpu.make_async_copy(
                source.at[:, pl.ds(pl.multiple_of(index * target.shape[2], target.shape[2]), target.shape[2])],
                target.at[slot],
                sems.at[slot, n],
            )
            for n, (source, target) in enumerate(pairs_of)
        ]

    table_load = pltpu.make_async_copy(table_hbm, table, table_sem)

    @pl.when(step == 0)
    def _():
        gain_ref[...] = jnp.zeros_like(gain_ref)
        table_load.start()
        for load in loads(0, 0):
            load.start()
        table_load.wait()

    for load in loads(step, now):
        load.wait()

    @pl.when(step + 1 < pl.num_programs(0))
    def _():
        for load in loads(step + 1, 1 - now):
            load.start()

    q_ref, og_ref, k_ref, v_ref = (two.at[now] for two in (q_two, og_two, k_two, v_two))
    slots = q_ref.shape[0]
    part = da_ref.shape[0]
    prefix = 2 * part
    total = prefix + slots
    scale = D ** (-0.5)
    log_scale = scale * math.log2(math.e)
    bf = jnp.bfloat16
    cosine, sine = table[0:slots, :], table[slots : 2 * slots, :]
    q_gain, k_gain = qg_ref[...], kg_ref[...]
    pairs = grouped // 2
    width = 2 * slots
    blocks = [slice(r, r + BLOCK) for r in range(0, total, BLOCK)]

    per = k_ref.shape[1] // D
    kept = []
    for h in range(per):
        here_h = slice(h * D, (h + 1) * D)
        key_n, key_hat, key_inv = norm_rope(k_ref[:, here_h], k_gain, cosine, sine)
        kept.append((key_hat, key_inv))
        for n, place in enumerate(places):
            piece = arrivals[2 * n].shape[0] // len(place)
            for source, row in enumerate(place):
                from_rows = slice(source * piece, (source + 1) * piece)
                keys[h, row : row + piece, :] = arrivals[2 * n][from_rows, here_h]
                vals[h, row : row + piece, :] = arrivals[2 * n + 1][from_rows, here_h]
        keys[h, prefix:total, :] = key_n
        vals[h, prefix:total, :] = v_ref[:, here_h]
        keys_t[h] = keys[h].T
        vals_t[h] = vals[h].T

    device = lax.axis_index("resp")
    length = jnp.int32(0)
    for n in range(lengths_ref.shape[1]):
        length = length + jnp.where(assign_ref[0, n] == device, lengths_ref[0, n], 0)
    live = lax.broadcasted_iota(jnp.int32, (slots, 1), 0) < length
    col1 = lax.broadcasted_iota(jnp.int32, (1, width), 1)
    slot1 = jnp.where(col1 >= slots, col1 - slots, col1)
    live_t = slot1 < length
    cols = lambda p: [slice((2 * p + j) * D, (2 * p + j + 1) * D) for j in range(2)]
    here = lambda p: slice((p % 2) * width, (p % 2 + 1) * width)
    state = [dict() for _ in range(per * pairs)]
    head = lambda p: p // pairs

    def prepare(p):
        st = state[p]
        st["prep"] = [norm_rope(q_ref[:, c], q_gain, cosine, sine) for c in cols(p)]
        st["query"] = jnp.concatenate([x[0] for x in st["prep"]], axis=0)
        grad = [jnp.where(live, og_ref[:, c].astype(jnp.float32), 0.0).astype(bf) for c in cols(p)]
        st["grad"] = jnp.concatenate(grad, axis=0)
        st["grad_t"] = st["grad"].T

    def multiply_in(p):
        st = state[p]
        top = jnp.full((8, width), MASKED, jnp.float32)
        for start in range(0, total, DOT):
            big = dot(keys[head(p), start : start + DOT, :], st["query"], NT)
            for off in range(0, DOT, BLOCK):
                rows = slice(start + off, start + off + BLOCK)
                s = big[off : off + BLOCK]
                if rows.start >= prefix:
                    row = lax.broadcasted_iota(jnp.int32, (BLOCK, width), 0) + (rows.start - prefix)
                    s = jnp.where(row <= slot1, s, MASKED)
                scores[p % 2, rows, :] = s
                top = jnp.maximum(top, fold_max(s))
        st["top"] = top
        for start in range(0, total, DOT):
            rows = slice(start, start + DOT)
            dprobs[p % 2, rows, :] = dot(vals[head(p), rows, :], st["grad"], NT)

    def soften(p):
        st = state[p]
        top = jnp.max(st["top"], axis=0, keepdims=True) * log_scale
        mass = jnp.zeros((8, width), jnp.float32)
        for rows in blocks:
            e = jnp.exp2(scores[p % 2, rows, :] * log_scale - top)
            scores[p % 2, rows, :] = e
            mass = mass + fold_rows(e)
        st["inv"] = 1.0 / jnp.sum(mass, axis=0, keepdims=True)
        for rows in blocks:
            probs[rows, here(p)] = (scores[p % 2, rows, :] * st["inv"]).astype(bf)

    def multiply_out(p):
        st = state[p]
        output = dot(vals_t[head(p)], probs[:, here(p)], NN)
        output = jnp.where(live_t, output, 0.0).astype(bf)
        st["rowdot"] = jnp.sum(output.astype(jnp.float32) * st["grad_t"].astype(jnp.float32), axis=0, keepdims=True)
        turned = output.T
        for j in range(2):
            out_ref[:, cols(p)[j]] = turned[j * slots : (j + 1) * slots]

    def value_grad(p):
        more = dot(probs[:, here(p)], state[p]["grad"], NN)
        acc_v[head(p)] = more if p % pairs == 0 else acc_v[head(p)] + more

    def score_grad(p):
        st = state[p]
        inv = st["inv"] * scale
        for rows in blocks:
            dscores[rows, here(p)] = (
                (scores[p % 2, rows, :] * inv) * (dprobs[p % 2, rows, :] - st["rowdot"])
            ).astype(bf)

    def query_key_grad(p):
        st = state[p]
        st["grad_qn"] = dot(keys_t[head(p)], dscores[:, here(p)], NN).T
        more = dot(dscores[:, here(p)], st["query"], NN)
        acc_k[head(p)] = more if p % pairs == 0 else acc_k[head(p)] + more

    def query_back(p):
        st = state[p]
        total_gain = jnp.zeros((8, D), jnp.float32)
        for j in range(2):
            back, by_hat = norm_rope_back(
                st["grad_qn"][j * slots : (j + 1) * slots], st["prep"][j][1], st["prep"][j][2], q_gain, cosine, sine
            )
            gq_ref[:, cols(p)[j]] = back.astype(bf)
            total_gain = total_gain + fold_rows(by_hat)
        gain_ref[0:8, :] += total_gain

    def finish(h):
        here_h = slice(h * D, (h + 1) * D)
        grad_kn, grad_vn = acc_k[h], acc_v[h]
        there_h = slice((per + h) * D, (per + h + 1) * D)
        da_ref[:, here_h] = grad_kn[:part]
        db_ref[:, here_h] = grad_kn[part:prefix].astype(bf)
        da_ref[:, there_h] = grad_vn[:part]
        db_ref[:, there_h] = grad_vn[part:prefix].astype(bf)
        gv_ref[:, here_h] = grad_vn[prefix:].astype(bf)
        back, by_hat = norm_rope_back(grad_kn[prefix:], kept[h][0], kept[h][1], k_gain, cosine, sine)
        gk_ref[:, here_h] = back.astype(bf)
        gain_ref[8:16, :] += fold_rows(by_hat)

    count = per * pairs
    prepare(0)
    multiply_in(0)
    for p in range(count):
        if p + 1 < count:
            prepare(p + 1)
        soften(p)
        if p + 1 < count:
            multiply_in(p + 1)
        if p > 0:
            query_key_grad(p - 1)
        multiply_out(p)
        value_grad(p)
        if p > 0:
            query_back(p - 1)
            if p % pairs == 0:
                finish(head(p - 1))
        score_grad(p)
    query_key_grad(count - 1)
    query_back(count - 1)
    finish(per - 1)


def attend(lengths, assign, q_gain, k_gain, queries, out_grad, keys, values, table, arrivals, places):
    slots, width = queries.shape
    kv_width = keys.shape[1]
    grouped = width // kv_width
    heads = kv_width // D
    part = sum(a.shape[0] for a in arrivals) // 2
    bf = jnp.bfloat16
    steps = heads // PER
    halves = []
    for a in arrivals:
        halves.append(pl.BlockSpec((a.shape[0], PER * D), lambda i: (0, i)))
        halves.append(pl.BlockSpec((a.shape[0], PER * D), lambda i: (0, steps + i)))
    whole = lambda shape: pl.BlockSpec(shape, lambda i: (0, 0))
    wide = pl.BlockSpec((slots, PER * grouped * D), lambda i: (0, i))
    thin = pl.BlockSpec((slots, PER * D), lambda i: (0, i))
    lead = pl.BlockSpec((part, 2 * PER * D), lambda i: (0, i))
    total = 2 * part + slots
    hbm = pl.BlockSpec(memory_space=pltpu.HBM)
    outs = [
        jax.ShapeDtypeStruct((slots, width), bf),
        jax.ShapeDtypeStruct((slots, width), bf),
        jax.ShapeDtypeStruct((slots, kv_width), bf),
        jax.ShapeDtypeStruct((slots, kv_width), bf),
        jax.ShapeDtypeStruct((part, 2 * kv_width), jnp.float32),
        jax.ShapeDtypeStruct((part, 2 * kv_width), bf),
        jax.ShapeDtypeStruct((16, D), jnp.float32),
    ]
    flops = 6 * 2 * heads * grouped * slots * D * total
    return pl.pallas_call(
        functools.partial(kernel, grouped=grouped, places=places),
        grid=(steps,),
        out_shape=outs,
        in_specs=[
            pl.BlockSpec(memory_space=pltpu.SMEM),
            pl.BlockSpec(memory_space=pltpu.SMEM),
            whole((1, D)), whole((1, D)),
            hbm, hbm, hbm, hbm, hbm,
        ] + halves,
        out_specs=[wide, wide, thin, thin, lead, lead, whole((16, D))],
        scratch_shapes=[
            pltpu.VMEM((PER, total, D), bf),
            pltpu.VMEM((PER, total, D), bf),
            pltpu.VMEM((PER, D, total), bf),
            pltpu.VMEM((PER, D, total), bf),
            pltpu.VMEM((2, total, 2 * slots), jnp.float32),
            pltpu.VMEM((2, total, 2 * slots), jnp.float32),
            pltpu.VMEM((total, 4 * slots), bf),
            pltpu.VMEM((total, 4 * slots), bf),
            pltpu.VMEM((PER, total, D), jnp.float32),
            pltpu.VMEM((PER, total, D), jnp.float32),
            pltpu.VMEM((2, slots, PER * grouped * D), bf),
            pltpu.VMEM((2, slots, PER * grouped * D), bf),
            pltpu.VMEM((2, slots, PER * D), bf),
            pltpu.VMEM((2, slots, PER * D), bf),
            pltpu.VMEM(table.shape, jnp.float32),
            pltpu.SemaphoreType.DMA((2, 4)),
            pltpu.SemaphoreType.DMA(()),
        ],
        compiler_params=pltpu.CompilerParams(
            dimension_semantics=("arbitrary",), vmem_limit_bytes=58 * 1024 * 1024
        ),
        cost_estimate=pl.CostEstimate(
            flops=2 * flops, bytes_accessed=heads * grouped * slots * D * 8, transcendentals=heads * grouped * slots * total
        ),
        name="attend",
    )(lengths, assign, q_gain, k_gain, queries, out_grad, keys, values, table, *[a for a in arrivals for _ in range(2)])


def moved(x, count, dz=0, dy=0, dc=0):
    ring = count // 4

    def target(i):
        z, y, c = i // (2 * ring), i // 2 % ring, i % 2
        return (z + dz) % 2 * 2 * ring + (y + dy) % ring * 2 + (c + dc) % 2

    return lax.ppermute(x, "resp", [(i, target(i)) for i in range(count)])


def first_fold(mine_ref, other_ref, own_ref, *parts):
    size = own_ref.shape[0]
    own_ref[...] = mine_ref[:size, :] + other_ref[:size, :].astype(jnp.float32)
    for n, part in enumerate(parts):
        rows = slice((n + 1) * size, (n + 2) * size)
        part[...] = (mine_ref[rows, :] + other_ref[rows, :].astype(jnp.float32)).astype(jnp.bfloat16)


def second_fold(own_ref, *rest):
    *parts, keep_ref, send_ref = rest
    size = keep_ref.shape[0]
    total = own_ref[...]
    for part in parts:
        total = total + part[...].astype(jnp.float32)
    keep_ref[...] = total[:size]
    send_ref[...] = total[size:].astype(jnp.bfloat16)


def last_fold(keep_ref, other_ref, keys_ref, vals_ref):
    span = PER * D
    total = (keep_ref[...] + other_ref[...].astype(jnp.float32)).astype(jnp.bfloat16)
    for n in range(keys_ref.shape[1] // span):
        here = slice(n * span, (n + 1) * span)
        keys_ref[:, here] = total[:, 2 * n * span : (2 * n + 1) * span]
        vals_ref[:, here] = total[:, (2 * n + 1) * span : (2 * n + 2) * span]


def small(body, name, steps, outs, *args):
    def block(shape):
        return pl.BlockSpec((shape[0], shape[1] // steps), lambda i: (0, i))

    return pl.pallas_call(
        body,
        grid=(steps,),
        out_shape=[jax.ShapeDtypeStruct(shape, kind) for shape, kind in outs],
        in_specs=[block(a.shape) for a in args],
        out_specs=[block(shape) for shape, _ in outs],
        compiler_params=pltpu.CompilerParams(vmem_limit_bytes=16 * 1024 * 1024),
        name=name,
    )(*args)


def shards(
    queries, keys, values, prefix_keys, prefix_values, out_grad, q_gain, k_gain, lengths, assign
):
    slots = queries.shape[1]
    count = lax.axis_size("resp")
    rows = prefix_keys.shape[1]
    ring = count // 4
    table = jnp.asarray(np.concatenate(tables(slots, rows * count), axis=0))
    f32, bf = jnp.float32, jnp.bfloat16
    width = keys.shape[2]

    mine = jnp.concatenate([prefix_keys[0], prefix_values[0]], axis=1)
    across = moved(mine, count, dz=1)
    pieces = {
        (z, y): moved((mine, across)[z], count, dy=y) if y else (mine, across)[z] for y in range(ring) for z in range(2)
    }
    half = 2 * ring * rows
    order = sorted(pieces)
    arrivals = [pieces[at] for at in order] + [moved(pieces[at], count, dc=1) for at in order]
    places = [[base + (2 * y + z) * rows] for base in (0, half) for z, y in order]

    attention, grad_q, grad_k, grad_v, mine_sum, other_sum, gains = attend(
        lengths, assign, q_gain.reshape(1, D), k_gain.reshape(1, D), queries[0], out_grad[0], keys[0], values[0], table, arrivals, places
    )
    pair = (2 * rows, 2 * width)
    other = moved(other_sum, count, dc=1)
    own, *parts = small(first_fold, "first_fold", 4, [(pair, f32)] + [(pair, bf)] * (ring - 1), mine_sum, other)
    parts = [moved(part, count, dy=ring - 1 - n) for n, part in enumerate(parts)]
    gains = jnp.sum(gains.reshape(2, 8, D), axis=1).reshape(1, 2 * D)
    devices = count * lax.axis_size("prompt")
    spread = lax.all_to_all(jnp.broadcast_to(gains, (devices, 2 * D)), ("prompt", "resp"), 0, 0)
    gains = jnp.sum(spread.reshape(devices, 2, D), axis=0)
    single = (rows, 2 * width)
    keep, send = small(second_fold, "second_fold", 1, [(single, f32), (single, bf)], own, *parts)
    other = moved(send, count, dz=1)
    pkeys, pvalues = small(last_fold, "last_fold", 1, [((rows, width), bf)] * 2, keep, other)
    return (
        attention[None],
        grad_q[None],
        grad_k[None],
        grad_v[None],
        pkeys[None],
        pvalues[None],
        gains[0],
        gains[1],
    )


def solution(mesh):
    rows = P("prompt", "resp", None)
    groups = P("prompt", None)
    return jax.shard_map(
        shards,
        mesh=mesh,
        in_specs=(rows, rows, rows, rows, rows, rows, P(), P(), groups, groups),
        out_specs=(rows, rows, rows, rows, rows, rows, P(), P()),
        check_vma=False,
    )
```

```python
import functools
import math

import jax
import jax.numpy as jnp
import numpy as np
from jax import lax
from jax.experimental import pallas as pl
from jax.experimental.pallas import tpu as pltpu
from jax.sharding import PartitionSpec as P

THETA = 1000000.0
EPS = 1e-06
MASKED = -1e30
D = 128
NT = (((1,), (1,)), ((), ()))
NN = (((1,), (0,)), ((), ()))
PER = 4
BLOCK = 64
DOT = 640


def dot(a, b, dims):
    return lax.dot_general(a, b, dims, preferred_element_type=jnp.float32)


def tables(slots, prefix):
    half = D // 2
    inverse = (THETA ** (-(np.arange(half, dtype=np.float32) * np.float32(2.0 / D)))).astype(np.float32)
    positions = (prefix + np.arange(slots)).astype(np.float32)
    angles = (positions[:, None] * inverse[None, :]).astype(np.float64)
    cosine, sine = np.cos(angles), np.sin(angles)
    return (
        np.concatenate([cosine, cosine], axis=1).astype(np.float32),
        np.concatenate([-sine, sine], axis=1).astype(np.float32),
    )


def swap(x):
    return pltpu.roll(x, D // 2, 1)


def norm_rope(raw, gain, cosine, sine):
    x = raw.astype(jnp.float32)
    inv = lax.rsqrt(jnp.mean(x * x, axis=1, keepdims=True) + EPS)
    hat = x * inv
    scaled = hat * gain
    return (scaled * cosine + swap(scaled) * sine).astype(jnp.bfloat16), hat, inv


def norm_rope_back(grad, hat, inv, gain, cosine, sine):
    back = grad * cosine - swap(grad) * sine
    by_hat = back * hat
    mean = jnp.mean(by_hat * gain, axis=1, keepdims=True)
    return inv * (back * gain - hat * mean), by_hat


def fold_rows(x):
    total = x[0:8]
    for start in range(8, x.shape[0], 8):
        total = total + x[start : start + 8]
    return total


def fold_max(x):
    total = x[0:8]
    for start in range(8, x.shape[0], 8):
        total = jnp.maximum(total, x[start : start + 8])
    return total


def kernel(
    lengths_ref, assign_ref, qg_ref, kg_ref, q_hbm, og_hbm, k_hbm, v_hbm, table_hbm,
    *rest,
    grouped, places,
):
    arrivals, rest = rest[: 2 * len(places)], rest[2 * len(places) :]
    (out_ref, gq_ref, gk_ref, gv_ref, da_ref, db_ref, gain_ref,
     keys, vals, keys_t, vals_t, scores, dprobs, probs, dscores, acc_k, acc_v,
     q_two, og_two, k_two, v_two, table, sems, table_sem) = rest
    step = pl.program_id(0)
    now = lax.rem(step, 2)

    def loads(index, slot):
        pairs_of = ((q_hbm, q_two), (og_hbm, og_two), (k_hbm, k_two), (v_hbm, v_two))
        return [
            pltpu.make_async_copy(
                source.at[:, pl.ds(pl.multiple_of(index * target.shape[2], target.shape[2]), target.shape[2])],
                target.at[slot],
                sems.at[slot, n],
            )
            for n, (source, target) in enumerate(pairs_of)
        ]

    table_load = pltpu.make_async_copy(table_hbm, table, table_sem)

    @pl.when(step == 0)
    def _():
        gain_ref[...] = jnp.zeros_like(gain_ref)
        table_load.start()
        for load in loads(0, 0):
            load.start()
        table_load.wait()

    for load in loads(step, now):
        load.wait()

    @pl.when(step + 1 < pl.num_programs(0))
    def _():
        for load in loads(step + 1, 1 - now):
            load.start()

    q_ref, og_ref, k_ref, v_ref = (two.at[now] for two in (q_two, og_two, k_two, v_two))
    slots = q_ref.shape[0]
    part = da_ref.shape[0]
    prefix = 2 * part
    total = prefix + slots
    scale = D ** (-0.5)
    log_scale = scale * math.log2(math.e)
    bf = jnp.bfloat16
    cosine, sine = table[0:slots, :], table[slots : 2 * slots, :]
    q_gain, k_gain = qg_ref[...], kg_ref[...]
    pairs = grouped // 2
    width = 2 * slots
    blocks = [slice(r, r + BLOCK) for r in range(0, total, BLOCK)]

    per = k_ref.shape[1] // D
    kept = []
    for h in range(per):
        here_h = slice(h * D, (h + 1) * D)
        key_n, key_hat, key_inv = norm_rope(k_ref[:, here_h], k_gain, cosine, sine)
        kept.append((key_hat, key_inv))
        for n, place in enumerate(places):
            piece = arrivals[2 * n].shape[0] // len(place)
            for source, row in enumerate(place):
                from_rows = slice(source * piece, (source + 1) * piece)
                keys[h, row : row + piece, :] = arrivals[2 * n][from_rows, here_h]
                vals[h, row : row + piece, :] = arrivals[2 * n + 1][from_rows, here_h]
        keys[h, prefix:total, :] = key_n
        vals[h, prefix:total, :] = v_ref[:, here_h]
        keys_t[h] = keys[h].T
        vals_t[h] = vals[h].T

    device = lax.axis_index("resp")
    length = jnp.int32(0)
    for n in range(lengths_ref.shape[1]):
        length = length + jnp.where(assign_ref[0, n] == device, lengths_ref[0, n], 0)
    live = lax.broadcasted_iota(jnp.int32, (slots, 1), 0) < length
    col1 = lax.broadcasted_iota(jnp.int32, (1, width), 1)
    slot1 = jnp.where(col1 >= slots, col1 - slots, col1)
    live_t = slot1 < length
    cols = lambda p: [slice((2 * p + j) * D, (2 * p + j + 1) * D) for j in range(2)]
    here = lambda p: slice((p % 2) * width, (p % 2 + 1) * width)
    state = [dict() for _ in range(per * pairs)]
    head = lambda p: p // pairs

    def prepare(p):
        st = state[p]
        st["prep"] = [norm_rope(q_ref[:, c], q_gain, cosine, sine) for c in cols(p)]
        st["query"] = jnp.concatenate([x[0] for x in st["prep"]], axis=0)
        grad = [jnp.where(live, og_ref[:, c].astype(jnp.float32), 0.0).astype(bf) for c in cols(p)]
        st["grad"] = jnp.concatenate(grad, axis=0)
        st["grad_t"] = st["grad"].T

    def multiply_in(p):
        st = state[p]
        top = jnp.full((8, width), MASKED, jnp.float32)
        for start in range(0, total, DOT):
            big = dot(keys[head(p), start : start + DOT, :], st["query"], NT)
            for off in range(0, DOT, BLOCK):
                rows = slice(start + off, start + off + BLOCK)
                s = big[off : off + BLOCK]
                if rows.start >= prefix:
                    row = lax.broadcasted_iota(jnp.int32, (BLOCK, width), 0) + (rows.start - prefix)
                    s = jnp.where(row <= slot1, s, MASKED)
                scores[p % 2, rows, :] = s
                top = jnp.maximum(top, fold_max(s))
        st["top"] = top
        for start in range(0, total, DOT):
            rows = slice(start, start + DOT)
            dprobs[p % 2, rows, :] = dot(vals[head(p), rows, :], st["grad"], NT)

    def soften(p):
        st = state[p]
        top = jnp.max(st["top"], axis=0, keepdims=True) * log_scale
        mass = jnp.zeros((8, width), jnp.float32)
        for rows in blocks:
            e = jnp.exp2(scores[p % 2, rows, :] * log_scale - top)
            scores[p % 2, rows, :] = e
            mass = mass + fold_rows(e)
        st["inv"] = 1.0 / jnp.sum(mass, axis=0, keepdims=True)
        for rows in blocks:
            probs[rows, here(p)] = (scores[p % 2, rows, :] * st["inv"]).astype(bf)

    def multiply_out(p):
        st = state[p]
        output = dot(vals_t[head(p)], probs[:, here(p)], NN)
        output = jnp.where(live_t, output, 0.0).astype(bf)
        st["rowdot"] = jnp.sum(output.astype(jnp.float32) * st["grad_t"].astype(jnp.float32), axis=0, keepdims=True)
        turned = output.T
        for j in range(2):
            out_ref[:, cols(p)[j]] = turned[j * slots : (j + 1) * slots]

    def value_grad(p):
        more = dot(probs[:, here(p)], state[p]["grad"], NN)
        acc_v[head(p)] = more if p % pairs == 0 else acc_v[head(p)] + more

    def score_grad(p):
        st = state[p]
        inv = st["inv"] * scale
        for rows in blocks:
            dscores[rows, here(p)] = (
                (scores[p % 2, rows, :] * inv) * (dprobs[p % 2, rows, :] - st["rowdot"])
            ).astype(bf)

    def query_key_grad(p):
        st = state[p]
        st["grad_qn"] = dot(keys_t[head(p)], dscores[:, here(p)], NN).T
        more = dot(dscores[:, here(p)], st["query"], NN)
        acc_k[head(p)] = more if p % pairs == 0 else acc_k[head(p)] + more

    def query_back(p):
        st = state[p]
        total_gain = jnp.zeros((8, D), jnp.float32)
        for j in range(2):
            back, by_hat = norm_rope_back(
                st["grad_qn"][j * slots : (j + 1) * slots], st["prep"][j][1], st["prep"][j][2], q_gain, cosine, sine
            )
            gq_ref[:, cols(p)[j]] = back.astype(bf)
            total_gain = total_gain + fold_rows(by_hat)
        gain_ref[0:8, :] += total_gain

    def finish(h):
        here_h = slice(h * D, (h + 1) * D)
        grad_kn, grad_vn = acc_k[h], acc_v[h]
        there_h = slice((per + h) * D, (per + h + 1) * D)
        da_ref[:, here_h] = grad_kn[:part]
        db_ref[:, here_h] = grad_kn[part:prefix].astype(bf)
        da_ref[:, there_h] = grad_vn[:part]
        db_ref[:, there_h] = grad_vn[part:prefix].astype(bf)
        gv_ref[:, here_h] = grad_vn[prefix:].astype(bf)
        back, by_hat = norm_rope_back(grad_kn[prefix:], kept[h][0], kept[h][1], k_gain, cosine, sine)
        gk_ref[:, here_h] = back.astype(bf)
        gain_ref[8:16, :] += fold_rows(by_hat)

    count = per * pairs
    prepare(0)
    multiply_in(0)
    for p in range(count):
        soften(p)
        if p + 1 < count:
            prepare(p + 1)
            multiply_in(p + 1)
        multiply_out(p)
        if p > 0:
            query_key_grad(p - 1)
        value_grad(p)
        if p > 0:
            query_back(p - 1)
            if p % pairs == 0:
                finish(head(p - 1))
        score_grad(p)
    query_key_grad(count - 1)
    query_back(count - 1)
    finish(per - 1)


def attend(lengths, assign, q_gain, k_gain, queries, out_grad, keys, values, table, arrivals, places):
    slots, width = queries.shape
    kv_width = keys.shape[1]
    grouped = width // kv_width
    heads = kv_width // D
    part = sum(a.shape[0] for a in arrivals) // 2
    bf = jnp.bfloat16
    steps = heads // PER
    halves = []
    for a in arrivals:
        halves.append(pl.BlockSpec((a.shape[0], PER * D), lambda i: (0, i)))
        halves.append(pl.BlockSpec((a.shape[0], PER * D), lambda i: (0, steps + i)))
    whole = lambda shape: pl.BlockSpec(shape, lambda i: (0, 0))
    wide = pl.BlockSpec((slots, PER * grouped * D), lambda i: (0, i))
    thin = pl.BlockSpec((slots, PER * D), lambda i: (0, i))
    lead = pl.BlockSpec((part, 2 * PER * D), lambda i: (0, i))
    total = 2 * part + slots
    hbm = pl.BlockSpec(memory_space=pltpu.HBM)
    outs = [
        jax.ShapeDtypeStruct((slots, width), bf),
        jax.ShapeDtypeStruct((slots, width), bf),
        jax.ShapeDtypeStruct((slots, kv_width), bf),
        jax.ShapeDtypeStruct((slots, kv_width), bf),
        jax.ShapeDtypeStruct((part, 2 * kv_width), jnp.float32),
        jax.ShapeDtypeStruct((part, 2 * kv_width), bf),
        jax.ShapeDtypeStruct((16, D), jnp.float32),
    ]
    flops = 6 * 2 * heads * grouped * slots * D * total
    return pl.pallas_call(
        functools.partial(kernel, grouped=grouped, places=places),
        grid=(steps,),
        out_shape=outs,
        in_specs=[
            pl.BlockSpec(memory_space=pltpu.SMEM),
            pl.BlockSpec(memory_space=pltpu.SMEM),
            whole((1, D)), whole((1, D)),
            hbm, hbm, hbm, hbm, hbm,
        ] + halves,
        out_specs=[wide, wide, thin, thin, lead, lead, whole((16, D))],
        scratch_shapes=[
            pltpu.VMEM((PER, total, D), bf),
            pltpu.VMEM((PER, total, D), bf),
            pltpu.VMEM((PER, D, total), bf),
            pltpu.VMEM((PER, D, total), bf),
            pltpu.VMEM((2, total, 2 * slots), jnp.float32),
            pltpu.VMEM((2, total, 2 * slots), jnp.float32),
            pltpu.VMEM((total, 4 * slots), bf),
            pltpu.VMEM((total, 4 * slots), bf),
            pltpu.VMEM((PER, total, D), jnp.float32),
            pltpu.VMEM((PER, total, D), jnp.float32),
            pltpu.VMEM((2, slots, PER * grouped * D), bf),
            pltpu.VMEM((2, slots, PER * grouped * D), bf),
            pltpu.VMEM((2, slots, PER * D), bf),
            pltpu.VMEM((2, slots, PER * D), bf),
            pltpu.VMEM(table.shape, jnp.float32),
            pltpu.SemaphoreType.DMA((2, 4)),
            pltpu.SemaphoreType.DMA(()),
        ],
        compiler_params=pltpu.CompilerParams(
            dimension_semantics=("arbitrary",), vmem_limit_bytes=58 * 1024 * 1024
        ),
        cost_estimate=pl.CostEstimate(
            flops=2 * flops, bytes_accessed=heads * grouped * slots * D * 8, transcendentals=heads * grouped * slots * total
        ),
        name="attend",
    )(lengths, assign, q_gain, k_gain, queries, out_grad, keys, values, table, *[a for a in arrivals for _ in range(2)])


def moved(x, count, dz=0, dy=0, dc=0):
    ring = count // 4

    def target(i):
        z, y, c = i // (2 * ring), i // 2 % ring, i % 2
        return (z + dz) % 2 * 2 * ring + (y + dy) % ring * 2 + (c + dc) % 2

    return lax.ppermute(x, "resp", [(i, target(i)) for i in range(count)])


def hold(mine_ref, own_ref, rest_ref):
    size = own_ref.shape[0]
    own_ref[...] = mine_ref[:size, :]
    rest_ref[...] = mine_ref[size:, :]


def first_fold(mine_ref, rest_ref, other_ref, own_ref, *parts):
    size = own_ref.shape[0]
    own_ref[...] = mine_ref[...] + other_ref[:size, :].astype(jnp.float32)
    for n, part in enumerate(parts):
        rows = slice(n * size, (n + 1) * size)
        there = slice((n + 1) * size, (n + 2) * size)
        part[...] = (rest_ref[rows, :] + other_ref[there, :].astype(jnp.float32)).astype(jnp.bfloat16)


def second_fold(own_ref, *rest):
    *parts, keep_ref, send_ref = rest
    size = keep_ref.shape[0]
    total = own_ref[...]
    for part in parts:
        total = total + part[...].astype(jnp.float32)
    keep_ref[...] = total[:size]
    send_ref[...] = total[size:].astype(jnp.bfloat16)


def last_fold(keep_ref, other_ref, keys_ref, vals_ref):
    span = PER * D
    total = (keep_ref[...] + other_ref[...].astype(jnp.float32)).astype(jnp.bfloat16)
    for n in range(keys_ref.shape[1] // span):
        here = slice(n * span, (n + 1) * span)
        keys_ref[:, here] = total[:, 2 * n * span : (2 * n + 1) * span]
        vals_ref[:, here] = total[:, (2 * n + 1) * span : (2 * n + 2) * span]


def small(body, name, steps, outs, *args):
    def block(shape):
        return pl.BlockSpec((shape[0], shape[1] // steps), lambda i: (0, i))

    return pl.pallas_call(
        body,
        grid=(steps,),
        out_shape=[jax.ShapeDtypeStruct(shape, kind) for shape, kind in outs],
        in_specs=[block(a.shape) for a in args],
        out_specs=[block(shape) for shape, _ in outs],
        compiler_params=pltpu.CompilerParams(vmem_limit_bytes=16 * 1024 * 1024),
        name=name,
    )(*args)


def shards(
    queries, keys, values, prefix_keys, prefix_values, out_grad, q_gain, k_gain, lengths, assign
):
    slots = queries.shape[1]
    count = lax.axis_size("resp")
    rows = prefix_keys.shape[1]
    ring = count // 4
    table = jnp.asarray(np.concatenate(tables(slots, rows * count), axis=0))
    f32, bf = jnp.float32, jnp.bfloat16
    width = keys.shape[2]

    mine = jnp.concatenate([prefix_keys[0], prefix_values[0]], axis=1)
    across = moved(mine, count, dz=1)
    pieces = {
        (z, y): moved((mine, across)[z], count, dy=y) if y else (mine, across)[z] for y in range(ring) for z in range(2)
    }
    half = 2 * ring * rows
    order = sorted(pieces)
    arrivals = [pieces[at] for at in order] + [moved(pieces[at], count, dc=1) for at in order]
    places = [[base + (2 * y + z) * rows] for base in (0, half) for z, y in order]

    attention, grad_q, grad_k, grad_v, mine_sum, other_sum, gains = attend(
        lengths, assign, q_gain.reshape(1, D), k_gain.reshape(1, D), queries[0], out_grad[0], keys[0], values[0], table, arrivals, places
    )
    pair = (2 * rows, 2 * width)
    other = moved(other_sum, count, dc=1)
    own, rest = small(hold, "hold", 4, [(pair, f32), ((2 * rows * (ring - 1), 2 * width), f32)], mine_sum)
    own, *parts = small(first_fold, "first_fold", 4, [(pair, f32)] + [(pair, bf)] * (ring - 1), own, rest, other)
    parts = [moved(part, count, dy=ring - 1 - n) for n, part in enumerate(parts)]
    gains = jnp.sum(gains.reshape(2, 8, D), axis=1).reshape(1, 2 * D)
    devices = count * lax.axis_size("prompt")
    spread = lax.all_to_all(jnp.broadcast_to(gains, (devices, 2 * D)), ("prompt", "resp"), 0, 0)
    gains = jnp.sum(spread.reshape(devices, 2, D), axis=0)
    single = (rows, 2 * width)
    keep, send = small(second_fold, "second_fold", 1, [(single, f32), (single, bf)], own, *parts)
    other = moved(send, count, dz=1)
    pkeys, pvalues = small(last_fold, "last_fold", 1, [((rows, width), bf)] * 2, keep, other)
    return (
        attention[None],
        grad_q[None],
        grad_k[None],
        grad_v[None],
        pkeys[None],
        pvalues[None],
        gains[0],
        gains[1],
    )


def solution(mesh):
    rows = P("prompt", "resp", None)
    groups = P("prompt", None)
    return jax.shard_map(
        shards,
        mesh=mesh,
        in_specs=(rows, rows, rows, rows, rows, rows, P(), P(), groups, groups),
        out_specs=(rows, rows, rows, rows, rows, rows, P(), P()),
        check_vma=False,
    )
```

```python
import functools
import math

import jax
import jax.numpy as jnp
import numpy as np
from jax import lax
from jax.experimental import pallas as pl
from jax.experimental.pallas import tpu as pltpu
from jax.sharding import PartitionSpec as P

THETA = 1000000.0
EPS = 1e-06
MASKED = -1e30
D = 128
NT = (((1,), (1,)), ((), ()))
NN = (((1,), (0,)), ((), ()))
PER = 4
BLOCK = 64
DOT = 640


def dot(a, b, dims):
    return lax.dot_general(a, b, dims, preferred_element_type=jnp.float32)


def tables(slots, prefix):
    half = D // 2
    inverse = (THETA ** (-(np.arange(half, dtype=np.float32) * np.float32(2.0 / D)))).astype(np.float32)
    positions = (prefix + np.arange(slots)).astype(np.float32)
    angles = (positions[:, None] * inverse[None, :]).astype(np.float64)
    cosine, sine = np.cos(angles), np.sin(angles)
    return (
        np.concatenate([cosine, cosine], axis=1).astype(np.float32),
        np.concatenate([-sine, sine], axis=1).astype(np.float32),
    )


def swap(x):
    return pltpu.roll(x, D // 2, 1)


def norm_rope(raw, gain, cosine, sine):
    x = raw.astype(jnp.float32)
    inv = lax.rsqrt(jnp.mean(x * x, axis=1, keepdims=True) + EPS)
    hat = x * inv
    scaled = hat * gain
    return (scaled * cosine + swap(scaled) * sine).astype(jnp.bfloat16), hat, inv


def norm_rope_back(grad, hat, inv, gain, cosine, sine):
    back = grad * cosine - swap(grad) * sine
    by_hat = back * hat
    mean = jnp.mean(by_hat * gain, axis=1, keepdims=True)
    return inv * (back * gain - hat * mean), by_hat


def fold_rows(x):
    total = x[0:8]
    for start in range(8, x.shape[0], 8):
        total = total + x[start : start + 8]
    return total


def fold_max(x):
    total = x[0:8]
    for start in range(8, x.shape[0], 8):
        total = jnp.maximum(total, x[start : start + 8])
    return total


def kernel(
    lengths_ref, assign_ref, qg_ref, kg_ref, q_hbm, og_hbm, k_hbm, v_hbm, table_hbm,
    *rest,
    grouped, places,
):
    arrivals, rest = rest[: 2 * len(places)], rest[2 * len(places) :]
    (out_ref, gq_ref, gk_ref, gv_ref, da_ref, db_ref, gain_ref,
     keys, vals, keys_t, vals_t, scores, dprobs, probs, dscores, acc_k, acc_v,
     q_two, og_two, k_two, v_two, table, sems, table_sem) = rest
    step = pl.program_id(0)
    now = lax.rem(step, 2)

    def loads(index, slot):
        pairs_of = ((q_hbm, q_two), (og_hbm, og_two), (k_hbm, k_two), (v_hbm, v_two))
        return [
            pltpu.make_async_copy(
                source.at[:, pl.ds(pl.multiple_of(index * target.shape[2], target.shape[2]), target.shape[2])],
                target.at[slot],
                sems.at[slot, n],
            )
            for n, (source, target) in enumerate(pairs_of)
        ]

    table_load = pltpu.make_async_copy(table_hbm, table, table_sem)

    @pl.when(step == 0)
    def _():
        gain_ref[...] = jnp.zeros_like(gain_ref)
        table_load.start()
        for load in loads(0, 0):
            load.start()
        table_load.wait()

    for load in loads(step, now):
        load.wait()

    @pl.when(step + 1 < pl.num_programs(0))
    def _():
        for load in loads(step + 1, 1 - now):
            load.start()

    q_ref, og_ref, k_ref, v_ref = (two.at[now] for two in (q_two, og_two, k_two, v_two))
    slots = q_ref.shape[0]
    part = da_ref.shape[0]
    prefix = 2 * part
    total = prefix + slots
    scale = D ** (-0.5)
    log_scale = scale * math.log2(math.e)
    bf = jnp.bfloat16
    cosine, sine = table[0:slots, :], table[slots : 2 * slots, :]
    q_gain, k_gain = qg_ref[...], kg_ref[...]
    pairs = grouped // 2
    width = 2 * slots
    blocks = [slice(r, r + BLOCK) for r in range(0, total, BLOCK)]

    per = k_ref.shape[1] // D
    kept = []
    for h in range(per):
        here_h = slice(h * D, (h + 1) * D)
        key_n, key_hat, key_inv = norm_rope(k_ref[:, here_h], k_gain, cosine, sine)
        kept.append((key_hat, key_inv))
        for n, place in enumerate(places):
            piece = arrivals[2 * n].shape[0] // len(place)
            for source, row in enumerate(place):
                from_rows = slice(source * piece, (source + 1) * piece)
                keys[h, row : row + piece, :] = arrivals[2 * n][from_rows, here_h]
                vals[h, row : row + piece, :] = arrivals[2 * n + 1][from_rows, here_h]
        keys[h, prefix:total, :] = key_n
        vals[h, prefix:total, :] = v_ref[:, here_h]
        keys_t[h] = keys[h].T
        vals_t[h] = vals[h].T

    device = lax.axis_index("resp")
    length = jnp.int32(0)
    for n in range(lengths_ref.shape[1]):
        length = length + jnp.where(assign_ref[0, n] == device, lengths_ref[0, n], 0)
    live = lax.broadcasted_iota(jnp.int32, (slots, 1), 0) < length
    col1 = lax.broadcasted_iota(jnp.int32, (1, width), 1)
    slot1 = jnp.where(col1 >= slots, col1 - slots, col1)
    live_t = slot1 < length
    cols = lambda p: [slice((2 * p + j) * D, (2 * p + j + 1) * D) for j in range(2)]
    here = lambda p: slice((p % 2) * width, (p % 2 + 1) * width)
    state = [dict() for _ in range(per * pairs)]
    head = lambda p: p // pairs

    def prepare(p):
        st = state[p]
        st["prep"] = [norm_rope(q_ref[:, c], q_gain, cosine, sine) for c in cols(p)]
        st["query"] = jnp.concatenate([x[0] for x in st["prep"]], axis=0)
        grad = [jnp.where(live, og_ref[:, c].astype(jnp.float32), 0.0).astype(bf) for c in cols(p)]
        st["grad"] = jnp.concatenate(grad, axis=0)
        st["grad_t"] = st["grad"].T

    def multiply_in(p):
        st = state[p]
        top = jnp.full((8, width), MASKED, jnp.float32)
        for start in range(0, total, DOT):
            big = dot(keys[head(p), start : start + DOT, :], st["query"], NT)
            for off in range(0, DOT, BLOCK):
                rows = slice(start + off, start + off + BLOCK)
                s = big[off : off + BLOCK]
                if rows.start >= prefix:
                    row = lax.broadcasted_iota(jnp.int32, (BLOCK, width), 0) + (rows.start - prefix)
                    s = jnp.where(row <= slot1, s, MASKED)
                scores[p % 2, rows, :] = s
                top = jnp.maximum(top, fold_max(s))
        st["top"] = top
        for start in range(0, total, DOT):
            rows = slice(start, start + DOT)
            dprobs[p % 2, rows, :] = dot(vals[head(p), rows, :], st["grad"], NT)

    def soften(p):
        st = state[p]
        top = jnp.max(st["top"], axis=0, keepdims=True) * log_scale
        mass = jnp.zeros((8, width), jnp.float32)
        for rows in blocks:
            e = jnp.exp2(scores[p % 2, rows, :] * log_scale - top)
            scores[p % 2, rows, :] = e
            mass = mass + fold_rows(e)
        st["inv"] = 1.0 / jnp.sum(mass, axis=0, keepdims=True)
        for rows in blocks:
            probs[rows, here(p)] = (scores[p % 2, rows, :] * st["inv"]).astype(bf)

    def multiply_out(p):
        st = state[p]
        output = dot(vals_t[head(p)], probs[:, here(p)], NN)
        output = jnp.where(live_t, output, 0.0).astype(bf)
        st["rowdot"] = jnp.sum(output.astype(jnp.float32) * st["grad_t"].astype(jnp.float32), axis=0, keepdims=True)
        turned = output.T
        for j in range(2):
            out_ref[:, cols(p)[j]] = turned[j * slots : (j + 1) * slots]

    def value_grad(p):
        more = dot(probs[:, here(p)], state[p]["grad"], NN)
        acc_v[head(p)] = more if p % pairs == 0 else acc_v[head(p)] + more

    def score_grad(p):
        st = state[p]
        inv = st["inv"] * scale
        for rows in blocks:
            dscores[rows, here(p)] = (
                (scores[p % 2, rows, :] * inv) * (dprobs[p % 2, rows, :] - st["rowdot"])
            ).astype(bf)

    def query_key_grad(p):
        st = state[p]
        st["grad_qn"] = dot(keys_t[head(p)], dscores[:, here(p)], NN).T
        more = dot(dscores[:, here(p)], st["query"], NN)
        acc_k[head(p)] = more if p % pairs == 0 else acc_k[head(p)] + more

    def query_back(p):
        st = state[p]
        total_gain = jnp.zeros((8, D), jnp.float32)
        for j in range(2):
            back, by_hat = norm_rope_back(
                st["grad_qn"][j * slots : (j + 1) * slots], st["prep"][j][1], st["prep"][j][2], q_gain, cosine, sine
            )
            gq_ref[:, cols(p)[j]] = back.astype(bf)
            total_gain = total_gain + fold_rows(by_hat)
        gain_ref[0:8, :] += total_gain

    def finish(h):
        here_h = slice(h * D, (h + 1) * D)
        grad_kn, grad_vn = acc_k[h], acc_v[h]
        there_h = slice((per + h) * D, (per + h + 1) * D)
        da_ref[:, here_h] = grad_kn[:part]
        db_ref[:, here_h] = grad_kn[part:prefix].astype(bf)
        da_ref[:, there_h] = grad_vn[:part]
        db_ref[:, there_h] = grad_vn[part:prefix].astype(bf)
        gv_ref[:, here_h] = grad_vn[prefix:].astype(bf)
        back, by_hat = norm_rope_back(grad_kn[prefix:], kept[h][0], kept[h][1], k_gain, cosine, sine)
        gk_ref[:, here_h] = back.astype(bf)
        gain_ref[8:16, :] += fold_rows(by_hat)

    count = per * pairs
    prepare(0)
    multiply_in(0)
    for p in range(count):
        soften(p)
        if p + 1 < count:
            prepare(p + 1)
            multiply_in(p + 1)
        multiply_out(p)
        if p > 0:
            query_key_grad(p - 1)
        value_grad(p)
        if p > 0:
            query_back(p - 1)
            if p % pairs == 0:
                finish(head(p - 1))
        score_grad(p)
    query_key_grad(count - 1)
    query_back(count - 1)
    finish(per - 1)


def attend(lengths, assign, q_gain, k_gain, queries, out_grad, keys, values, table, arrivals, places):
    slots, width = queries.shape
    kv_width = keys.shape[1]
    grouped = width // kv_width
    heads = kv_width // D
    part = sum(a.shape[0] for a in arrivals) // 2
    bf = jnp.bfloat16
    steps = heads // PER
    halves = []
    for a in arrivals:
        halves.append(pl.BlockSpec((a.shape[0], PER * D), lambda i: (0, i)))
        halves.append(pl.BlockSpec((a.shape[0], PER * D), lambda i: (0, steps + i)))
    whole = lambda shape: pl.BlockSpec(shape, lambda i: (0, 0))
    wide = pl.BlockSpec((slots, PER * grouped * D), lambda i: (0, i))
    thin = pl.BlockSpec((slots, PER * D), lambda i: (0, i))
    lead = pl.BlockSpec((part, 2 * PER * D), lambda i: (0, i))
    total = 2 * part + slots
    hbm = pl.BlockSpec(memory_space=pltpu.HBM)
    outs = [
        jax.ShapeDtypeStruct((slots, width), bf),
        jax.ShapeDtypeStruct((slots, width), bf),
        jax.ShapeDtypeStruct((slots, kv_width), bf),
        jax.ShapeDtypeStruct((slots, kv_width), bf),
        jax.ShapeDtypeStruct((part, 2 * kv_width), jnp.float32),
        jax.ShapeDtypeStruct((part, 2 * kv_width), bf),
        jax.ShapeDtypeStruct((16, D), jnp.float32),
    ]
    flops = 6 * 2 * heads * grouped * slots * D * total
    return pl.pallas_call(
        functools.partial(kernel, grouped=grouped, places=places),
        grid=(steps,),
        out_shape=outs,
        in_specs=[
            pl.BlockSpec(memory_space=pltpu.SMEM),
            pl.BlockSpec(memory_space=pltpu.SMEM),
            whole((1, D)), whole((1, D)),
            hbm, hbm, hbm, hbm, hbm,
        ] + halves,
        out_specs=[wide, wide, thin, thin, lead, lead, whole((16, D))],
        scratch_shapes=[
            pltpu.VMEM((PER, total, D), bf),
            pltpu.VMEM((PER, total, D), bf),
            pltpu.VMEM((PER, D, total), bf),
            pltpu.VMEM((PER, D, total), bf),
            pltpu.VMEM((2, total, 2 * slots), jnp.float32),
            pltpu.VMEM((2, total, 2 * slots), jnp.float32),
            pltpu.VMEM((total, 4 * slots), bf),
            pltpu.VMEM((total, 4 * slots), bf),
            pltpu.VMEM((PER, total, D), jnp.float32),
            pltpu.VMEM((PER, total, D), jnp.float32),
            pltpu.VMEM((2, slots, PER * grouped * D), bf),
            pltpu.VMEM((2, slots, PER * grouped * D), bf),
            pltpu.VMEM((2, slots, PER * D), bf),
            pltpu.VMEM((2, slots, PER * D), bf),
            pltpu.VMEM(table.shape, jnp.float32),
            pltpu.SemaphoreType.DMA((2, 4)),
            pltpu.SemaphoreType.DMA(()),
        ],
        compiler_params=pltpu.CompilerParams(
            dimension_semantics=("arbitrary",), vmem_limit_bytes=58 * 1024 * 1024
        ),
        cost_estimate=pl.CostEstimate(
            flops=2 * flops, bytes_accessed=heads * grouped * slots * D * 8, transcendentals=heads * grouped * slots * total
        ),
        name="attend",
    )(lengths, assign, q_gain, k_gain, queries, out_grad, keys, values, table, *[a for a in arrivals for _ in range(2)])


def moved(x, count, dz=0, dy=0, dc=0):
    ring = count // 4

    def target(i):
        z, y, c = i // (2 * ring), i // 2 % ring, i % 2
        return (z + dz) % 2 * 2 * ring + (y + dy) % ring * 2 + (c + dc) % 2

    return lax.ppermute(x, "resp", [(i, target(i)) for i in range(count)])


def hold(mine_ref, own_ref, rest_ref):
    size = own_ref.shape[0]
    own_ref[...] = mine_ref[:size, :]
    rest_ref[...] = mine_ref[size:, :]


def first_fold(mine_ref, rest_ref, other_ref, gain_ref, gain_other_ref, own_ref, *outs):
    *parts, gain_sum_ref = outs
    gain_sum_ref[...] = gain_ref[...] + gain_other_ref[...]
    size = own_ref.shape[0]
    own_ref[...] = mine_ref[...] + other_ref[:size, :].astype(jnp.float32)
    for n, part in enumerate(parts):
        rows = slice(n * size, (n + 1) * size)
        there = slice((n + 1) * size, (n + 2) * size)
        part[...] = (rest_ref[rows, :] + other_ref[there, :].astype(jnp.float32)).astype(jnp.bfloat16)


def second_fold(own_ref, *rest):
    *parts, keep_ref, send_ref = rest
    size = keep_ref.shape[0]
    total = own_ref[...]
    for part in parts:
        total = total + part[...].astype(jnp.float32)
    keep_ref[...] = total[:size]
    send_ref[...] = total[size:].astype(jnp.bfloat16)


def last_fold(keep_ref, other_ref, keys_ref, vals_ref):
    span = PER * D
    total = (keep_ref[...] + other_ref[...].astype(jnp.float32)).astype(jnp.bfloat16)
    for n in range(keys_ref.shape[1] // span):
        here = slice(n * span, (n + 1) * span)
        keys_ref[:, here] = total[:, 2 * n * span : (2 * n + 1) * span]
        vals_ref[:, here] = total[:, (2 * n + 1) * span : (2 * n + 2) * span]


def small(body, name, steps, outs, *args):
    def block(shape):
        return pl.BlockSpec((shape[0], shape[1] // steps), lambda i: (0, i))

    return pl.pallas_call(
        body,
        grid=(steps,),
        out_shape=[jax.ShapeDtypeStruct(shape, kind) for shape, kind in outs],
        in_specs=[block(a.shape) for a in args],
        out_specs=[block(shape) for shape, _ in outs],
        compiler_params=pltpu.CompilerParams(vmem_limit_bytes=16 * 1024 * 1024),
        name=name,
    )(*args)


def shards(
    queries, keys, values, prefix_keys, prefix_values, out_grad, q_gain, k_gain, lengths, assign
):
    slots = queries.shape[1]
    count = lax.axis_size("resp")
    rows = prefix_keys.shape[1]
    ring = count // 4
    table = jnp.asarray(np.concatenate(tables(slots, rows * count), axis=0))
    f32, bf = jnp.float32, jnp.bfloat16
    width = keys.shape[2]

    mine = jnp.concatenate([prefix_keys[0], prefix_values[0]], axis=1)
    across = moved(mine, count, dz=1)
    pieces = {
        (z, y): moved((mine, across)[z], count, dy=y) if y else (mine, across)[z] for y in range(ring) for z in range(2)
    }
    half = 2 * ring * rows
    order = sorted(pieces)
    arrivals = [pieces[at] for at in order] + [moved(pieces[at], count, dc=1) for at in order]
    places = [[base + (2 * y + z) * rows] for base in (0, half) for z, y in order]

    attention, grad_q, grad_k, grad_v, mine_sum, other_sum, gains = attend(
        lengths, assign, q_gain.reshape(1, D), k_gain.reshape(1, D), queries[0], out_grad[0], keys[0], values[0], table, arrivals, places
    )
    pair = (2 * rows, 2 * width)
    other = moved(other_sum, count, dc=1)
    own, rest = small(hold, "hold", 1, [(pair, f32), ((2 * rows * (ring - 1), 2 * width), f32)], mine_sum)
    own, *parts, gains = small(
        first_fold, "first_fold", 1, [(pair, f32)] + [(pair, bf)] * (ring - 1) + [(gains.shape, f32)],
        own, rest, other, gains, moved(gains, count, dc=1),
    )
    parts = [moved(part, count, dy=ring - 1 - n) for n, part in enumerate(parts)]
    gains = jnp.sum(gains.reshape(2, 8, D), axis=1).reshape(1, 2 * D)
    devices = count * lax.axis_size("prompt")
    same_core = [list(range(core, devices, 2)) for core in range(2)]
    spread = lax.all_to_all(
        jnp.broadcast_to(gains, (devices // 2, 2 * D)), ("prompt", "resp"), 0, 0, axis_index_groups=same_core
    )
    gains = jnp.sum(spread.reshape(devices // 2, 2, D), axis=0)
    single = (rows, 2 * width)
    keep, send = small(second_fold, "second_fold", 1, [(single, f32), (single, bf)], own, *parts)
    other = moved(send, count, dz=1)
    pkeys, pvalues = small(last_fold, "last_fold", 1, [((rows, width), bf)] * 2, keep, other)
    return (
        attention[None],
        grad_q[None],
        grad_k[None],
        grad_v[None],
        pkeys[None],
        pvalues[None],
        gains[0],
        gains[1],
    )


def solution(mesh):
    rows = P("prompt", "resp", None)
    groups = P("prompt", None)
    return jax.shard_map(
        shards,
        mesh=mesh,
        in_specs=(rows, rows, rows, rows, rows, rows, P(), P(), groups, groups),
        out_specs=(rows, rows, rows, rows, rows, rows, P(), P()),
        check_vma=False,
    )
```
